512 devices in a mesh: dp: 2 (over y_lo), cand: 32 (over z, y_hi), tensor: 8 (over x, core).
Axes of the slice: x: 4, y: 8 (y_hi: 4, y_lo: 2; y = y_hi * 2 + y_lo), z: 8, core: 2. Of those that a mesh axis runs over, the one named last changes fastest.
Arguments:
- cand_query: bfloat16 [2, 64, 128, 4096], P('dp', 'cand', None, 'tensor'), may hold values from -88 to 88
- cand_key: bfloat16 [2, 64, 128, 1024], P('dp', 'cand', None, 'tensor'), may hold values from -4 to 4
- shared_prefix_key: bfloat16 [2, 1024, 1024], P('dp', 'cand', 'tensor'), may hold values from -4 to 4
- cand_hidden: bfloat16 [2, 64, 128, 4096], P('dp', 'cand', 'tensor'), may hold values from -6 to 6
- prefix_hidden: bfloat16 [2, 1024, 4096], P('dp', ('cand', 'tensor')), may hold values from -6 to 6
- value_matrix: bfloat16 [4096, 1024], P(None, 'tensor'), may hold values from -0.09375 to 0.09375
- out_cotangent: bfloat16 [2, 64, 128, 4096], P('dp', 'cand', None, 'tensor'), may hold values from -96 to 96
- cand_scores: float32 [2, 64], P('dp', 'cand'), may hold values from -15 to 315
- ranking: int32 [2, 64], P('dp'), may hold values from 0 to 63, each once within a row
- lengths: int32 [2, 64], P('dp', 'cand'), may hold values from 2 to 128, as said below
Outputs:
- grad_query: bfloat16 [2, 64, 128, 4096], P('dp', 'cand', None, 'tensor')
- grad_cand_key: bfloat16 [2, 64, 128, 1024], P('dp', 'cand', None, 'tensor')
- grad_prefix_key: bfloat16 [2, 1024, 1024], P('dp', 'cand', 'tensor')
- grad_prefix_value: bfloat16 [2, 1024, 1024], P('dp', 'cand', 'tensor')
- grad_value_weight: float32 [4096, 1024], P(('dp', 'cand'), 'tensor')
The draws below stay inside these ranges and needn't reach their ends.
Inputs may be any that keep to these rules, and one draw needn't show every extreme that they name: `lengths`: every list has a candidate of exactly 128 tokens.
All inputs are finite; a program needn't handle non-finite values.
Results may differ from the reference program's by a relative error of at most 0.012.
Values may be sent and summed in bfloat16 or wider, within the bound.
A program may use at most 64 MiB of HBM per device.

```python
import jax
import jax.numpy as jnp
from jax import lax

MODEL_DIM = 4096
QUERY_HEADS = 32
KEY_VALUE_HEADS = 8
HEAD_SIZE = 128
PREFIX_LENGTH = 1024
CANDIDATE_LENGTH = 128
CANDIDATE_COUNT = 64
LIST_COUNT = 2


def base_keys(key):
    return jnp.clip(jax.random.normal(key, (LIST_COUNT, CANDIDATE_COUNT, CANDIDATE_LENGTH, KEY_VALUE_HEADS * HEAD_SIZE), jnp.float32), -4.0, 4.0)


def draw_cand_key(key, part):
    base_values = base_keys(key)
    return base_values.astype(jnp.bfloat16)


def draw_cand_query(key, part):
    key = jax.random.fold_in(key, 5)
    queries = jnp.clip(jax.random.normal(key, (LIST_COUNT, CANDIDATE_COUNT, CANDIDATE_LENGTH, QUERY_HEADS * HEAD_SIZE), jnp.float32), -4.0, 4.0)
    return queries.astype(jnp.bfloat16)


def draw_cand_scores(key, part):
    key = jax.random.fold_in(key, 11)
    base_values = jnp.clip(3.0 * jax.random.normal(key, (LIST_COUNT, CANDIDATE_COUNT), jnp.float32), -15.0, 15.0)
    return base_values


def draw_lengths(key, part):
    key = jax.random.fold_in(key, 7)
    key_lengths, key_longest = jax.random.split(key)
    drawn_lengths = jax.random.randint(key_lengths, (LIST_COUNT, CANDIDATE_COUNT), 2, CANDIDATE_LENGTH + 1)
    chosen = jax.random.randint(key_longest, (LIST_COUNT, 1), 0, CANDIDATE_COUNT)
    longest = jnp.arange(CANDIDATE_COUNT)[None, :] == chosen
    return jnp.where(longest, CANDIDATE_LENGTH, drawn_lengths).astype(jnp.int32)


def level_of(own_key, extent, shards, smallest, largest):
    gain, own = 1.0, jax.random.fold_in(own_key, 6)
    for dim, shards_of in shards:
        heights = jnp.exp(jax.random.uniform(jax.random.fold_in(own, dim), (shards_of,), jnp.float32, smallest / len(shards), largest / len(shards)))
        gain = gain * jnp.repeat(heights, extent[dim] // shards_of).reshape([-1 if axis == dim else 1 for axis in range(len(extent))])
    return gain


def bell_draw(rng, dims, scale, most, shards=(), held_as=jnp.bfloat16):
    entries = scale * jax.random.normal(rng, dims, jnp.float32)
    if shards:
        entries = entries * level_of(rng, dims, shards, -0.22, 0.18)
    return jnp.clip(entries, -most, most).astype(held_as)


def setup_inputs(seed: int = 0) -> dict:
    seeds = jax.random.split(jax.random.key(seed), 11)
    cand_query = draw_cand_query(jax.random.fold_in(seeds[10], 71), 0)
    cand_key = draw_cand_key(jax.random.fold_in(seeds[10], 71), 0)
    shared_prefix_key = bell_draw(seeds[2], (LIST_COUNT, PREFIX_LENGTH, KEY_VALUE_HEADS * HEAD_SIZE), 1.0, 4.0, ((0, 2), (1, 32), (2, 8)))
    cand_hidden = bell_draw(seeds[3], (LIST_COUNT, CANDIDATE_COUNT, CANDIDATE_LENGTH, MODEL_DIM), 1.0, 6.0, ((0, 2), (1, 32), (2, 8)))
    prefix_hidden = bell_draw(seeds[4], (LIST_COUNT, PREFIX_LENGTH, MODEL_DIM), 1.0, 6.0, ((0, 2), (1, 256)))
    value_matrix = bell_draw(seeds[5], (MODEL_DIM, KEY_VALUE_HEADS * HEAD_SIZE), MODEL_DIM ** -0.5, 0.09375, ((1, 8),))
    out_cotangent = bell_draw(seeds[6], (LIST_COUNT, CANDIDATE_COUNT, CANDIDATE_LENGTH, QUERY_HEADS * HEAD_SIZE), 16.0, 96.0, ((0, 2), (1, 32), (3, 8)))
    cand_scores = draw_cand_scores(jax.random.fold_in(seeds[10], 71), 0)
    ranking = jax.vmap(lambda own: jax.random.permutation(own, CANDIDATE_COUNT))(jax.random.split(seeds[8], LIST_COUNT)).reshape((LIST_COUNT, CANDIDATE_COUNT)).astype(jnp.int32)
    lengths = draw_lengths(jax.random.fold_in(seeds[10], 71), 0)
    return dict(cand_query=cand_query, cand_key=cand_key, shared_prefix_key=shared_prefix_key, cand_hidden=cand_hidden, prefix_hidden=prefix_hidden, value_matrix=value_matrix, out_cotangent=out_cotangent, cand_scores=cand_scores, ranking=ranking, lengths=lengths)


def listwise_loss(scores, ranking):
    ordered = jnp.take_along_axis(scores, ranking, axis=1)
    total_ranks = ordered.shape[1]
    rank_rows = jnp.arange(total_ranks, dtype=jnp.int32)
    later_mask = rank_rows[None, :] >= rank_rows[:, None]
    masked = jnp.where(later_mask[None], ordered[:, None, :], -jnp.inf)
    return jnp.sum(jax.nn.logsumexp(masked, axis=2) - ordered)

def attend(queries, key_self, value_self, cot_rows, length, prefix_keys, prefix_values):
    cand_len = queries.shape[0]
    prefix_len = prefix_keys.shape[0]
    kv_heads = key_self.shape[1] // HEAD_SIZE
    heads_per_group = queries.shape[1] // (kv_heads * HEAD_SIZE)
    inv_root = HEAD_SIZE ** (-0.5)
    all_keys = jnp.concatenate([prefix_keys, key_self], 0).reshape(prefix_len + cand_len, kv_heads, HEAD_SIZE)
    all_values = jnp.concatenate([prefix_values, value_self], 0).reshape(prefix_len + cand_len, kv_heads, HEAD_SIZE)
    query_heads = queries.reshape(cand_len, kv_heads, heads_per_group, HEAD_SIZE).astype(jnp.float32)
    cot_heads = cot_rows.reshape(cand_len, kv_heads, heads_per_group, HEAD_SIZE).astype(jnp.float32)
    keys_wide = all_keys.astype(jnp.float32)
    logits = jnp.einsum('tgrd,jgd->grtj', query_heads, keys_wide) * inv_root
    position = jnp.arange(cand_len, dtype=jnp.int32)[:, None]
    slot = jnp.arange(prefix_len + cand_len, dtype=jnp.int32)[None, :] - prefix_len
    allowed = (slot < 0) | (slot <= position) & (slot < length)
    logits = jnp.where(allowed, logits, -jnp.inf)
    probabilities = jax.nn.softmax(logits, axis=-1)
    probs_low = probabilities.astype(jnp.bfloat16).astype(jnp.float32)
    dprob = jnp.einsum('tgrd,jgd->grtj', cot_heads, all_values.astype(jnp.float32))
    row_total = lax.optimization_barrier(jnp.sum(probabilities * dprob, axis=-1, keepdims=True))
    dscore = (probabilities * (dprob - row_total)).astype(jnp.bfloat16).astype(jnp.float32)
    grad_q = (jnp.einsum('grtj,jgd->tgrd', dscore, keys_wide) * inv_root).astype(jnp.bfloat16)
    grad_k = jnp.einsum('grtj,tgrd->jgd', dscore, query_heads) * inv_root
    grad_v = jnp.einsum('grtj,tgrd->jgd', probs_low, cot_heads)
    key_value_width = kv_heads * HEAD_SIZE
    return (grad_q.reshape(cand_len, -1), grad_k[prefix_len:].reshape(cand_len, key_value_width).astype(jnp.bfloat16), grad_v[prefix_len:].reshape(cand_len, key_value_width).astype(jnp.bfloat16), grad_k[:prefix_len].reshape(prefix_len, key_value_width), grad_v[:prefix_len].reshape(prefix_len, key_value_width))

def reference(cand_query, cand_key, shared_prefix_key, cand_hidden, prefix_hidden, value_matrix, out_cotangent, cand_scores, ranking, lengths):
    key_value_width = KEY_VALUE_HEADS * HEAD_SIZE
    score_grad = jax.grad(listwise_loss)(cand_scores, ranking)
    cand_value = jnp.dot(cand_hidden.reshape(-1, MODEL_DIM), value_matrix, preferred_element_type=jnp.float32).astype(jnp.bfloat16).reshape(LIST_COUNT, CANDIDATE_COUNT, CANDIDATE_LENGTH, key_value_width)
    prefix_value = jnp.dot(prefix_hidden.reshape(-1, MODEL_DIM), value_matrix, preferred_element_type=jnp.float32).astype(jnp.bfloat16).reshape(LIST_COUNT, PREFIX_LENGTH, key_value_width)
    live_mask = (jnp.arange(CANDIDATE_LENGTH, dtype=jnp.int32)[None, None, :] < lengths[:, :, None]).astype(jnp.float32)
    cotangent = (out_cotangent.astype(jnp.float32) * score_grad[:, :, None, None] * live_mask[..., None]).astype(jnp.bfloat16)
    total_items = LIST_COUNT * CANDIDATE_COUNT

    def per_item(prefix_acc, scanned):
        item_index, queries, key_self, value_self, cot_rows, length = scanned
        list_index = item_index // CANDIDATE_COUNT
        keys_here = lax.dynamic_index_in_dim(shared_prefix_key, list_index, 0, keepdims=False)
        values_here = lax.dynamic_index_in_dim(prefix_value, list_index, 0, keepdims=False)
        grad_q, grad_k, grad_v, pre_key, pre_value = attend(queries, key_self, value_self, cot_rows, length, keys_here, values_here)
        current = lax.dynamic_index_in_dim(prefix_acc, list_index, 0, keepdims=False)
        prefix_acc = lax.dynamic_update_index_in_dim(prefix_acc, current + jnp.stack([pre_key, pre_value], 0), list_index, 0)
        return (prefix_acc, (grad_q, grad_k, grad_v))
    zero_terms = jnp.zeros((LIST_COUNT, 2, PREFIX_LENGTH, key_value_width), jnp.float32)
    scanned = (jnp.arange(total_items, dtype=jnp.int32), cand_query.reshape(total_items, CANDIDATE_LENGTH, QUERY_HEADS * HEAD_SIZE), cand_key.reshape(total_items, CANDIDATE_LENGTH, key_value_width), cand_value.reshape(total_items, CANDIDATE_LENGTH, key_value_width), cotangent.reshape(total_items, CANDIDATE_LENGTH, QUERY_HEADS * HEAD_SIZE), lengths.reshape(total_items))
    prefix_terms, (grad_q, grad_k, cand_dv) = lax.scan(per_item, zero_terms, scanned)
    grad_prefix_key = prefix_terms[:, 0].astype(jnp.bfloat16)
    grad_prefix_value = prefix_terms[:, 1].astype(jnp.bfloat16)
    grad_value_weight = jnp.dot(prefix_hidden.reshape(-1, MODEL_DIM).T, grad_prefix_value.reshape(-1, key_value_width), preferred_element_type=jnp.float32)
    grad_value_weight = grad_value_weight + jnp.dot(cand_hidden.reshape(-1, MODEL_DIM).T, cand_dv.reshape(-1, key_value_width), preferred_element_type=jnp.float32)
    return (grad_q.reshape(LIST_COUNT, CANDIDATE_COUNT, CANDIDATE_LENGTH, QUERY_HEADS * HEAD_SIZE), grad_k.reshape(LIST_COUNT, CANDIDATE_COUNT, CANDIDATE_LENGTH, key_value_width), grad_prefix_key, grad_prefix_value, grad_value_weight)
```

```python
import jax
import jax.numpy as jnp
from jax import lax
from jax.experimental import pallas as pl
from jax.experimental.pallas import tpu as pltpu
from jax.sharding import PartitionSpec as P

MESH = pl.DeviceIdType.MESH
BF16, F32 = jnp.bfloat16, jnp.float32
NZ, NYH, NY, NX, NT = 8, 4, 8, 4, 8
HEAD = 128
PREFIX = 1024
CAND = 128
CHUNK = 256
WIDTH = 4096
INV_ROOT = HEAD ** (-0.5)


def dot(a, b):
    return lax.dot_general(a, b, (((1,), (0,)), ((), ())), preferred_element_type=F32)


def dot_nt(a, b):
    return lax.dot_general(a, b, (((1,), (1,)), ((), ())), preferred_element_type=F32)


class Exchange:
    def __init__(self, n, me, device, src, dst, sems):
        self.n, self.me, self.device, self.src, self.dst, self.sems = n, me, device, src, dst, sems

    def copy(self, k, slot):
        peer = lax.rem(self.me + k, self.n)
        return pltpu.make_async_remote_copy(
            src_ref=self.src(peer),
            dst_ref=self.dst(slot),
            send_sem=self.sems.at[0, k],
            recv_sem=self.sems.at[1, k],
            device_id=self.device(peer),
            device_id_type=MESH,
        )

    def loop(self, step):
        def body(k, carry):
            step(k)
            return carry

        lax.fori_loop(1, self.n, body, 0)

    def start(self):
        self.loop(lambda k: self.copy(k, self.me).start())

    def wait_recv(self):
        self.loop(lambda k: self.copy(k, lax.rem(self.me + self.n - k, self.n)).wait_recv())

    def wait_send(self):
        self.loop(lambda k: self.copy(k, self.me).wait_send())


def rank_gradient(scores_row, ranking_row):
    n = ranking_row.shape[1]
    rows = lax.broadcasted_iota(jnp.int32, (n, n), 0)
    cols = lax.broadcasted_iota(jnp.int32, (n, n), 1)
    scores_col = jnp.sum(jnp.where(rows == cols, scores_row, 0.0), axis=1, keepdims=True)
    picker = ranking_row == rows
    ordered = jnp.sum(jnp.where(picker, scores_col, 0.0), axis=0, keepdims=True)
    later = cols >= rows
    masked = jnp.where(later, ordered, -jnp.inf)
    top = jnp.max(masked, axis=1, keepdims=True)
    weights = jnp.exp(masked - top)
    suffix = weights / jnp.sum(weights, axis=1, keepdims=True)
    by_rank = jnp.sum(suffix, axis=0, keepdims=True) - 1.0
    return jnp.sum(jnp.where(picker, by_rank, 0.0), axis=1, keepdims=True)


def kernel(
    q_ref, ck_ref, pk_ref, ch_ref, ph_ref, w_ref, oc_ref, sc_ref, rk_ref, ln_ref,
    gq_ref, gck_ref, gpk_ref, gpv_ref, gw_ref,
    hc_ref, hp_ref, kall_ref, vall_ref, kt_ref, s1_ref, s2_ref,
    qs_ref, cs_ref, p_ref, vc_ref, dvp_ref, dvc_ref, dkp_ref, dkc_ref, dvr_ref,
    send_v, send_k, rva1, rvb1, rva2, rvb2, rka1, rkb1, rka2, rkb2, tva2, tvb2, tka2, tkb2,
    send_w, rwa1, rwb1, rwa2, rwb2, twa2, twb2,
    sem_hp, sem_hx, sem_hs, sem_s, sem_k, sem_v, sem_dv, sem_dk, sem_dw,
):
    dp = lax.axis_index("dp")
    cand = lax.axis_index("cand")
    tens = lax.axis_index("tensor")
    z, yh = cand // NYH, lax.rem(cand, NYH)
    y = dp * NYH + yh
    x, core = tens // 2, lax.rem(tens, 2)
    other = 1 - core

    def at_t(t):
        return (dp, cand, t)

    def at_x(xx):
        return (dp, cand, xx * 2 + core)

    def at_z(zz):
        return (dp, zz * NYH + yh, tens)

    def at_yh(yy):
        return (dp, z * NYH + yy, tens)

    def at_y(yy):
        return (yy // NYH, z * NYH + lax.rem(yy, NYH), tens)

    barrier = pltpu.get_barrier_semaphore()
    for n, me, device in ((NT, tens, at_t), (NZ, z, at_z), (NY, y, at_y)):
        def greet(k, carry, n=n, me=me, device=device):
            pl.semaphore_signal(
                barrier, inc=1, device_id=device(lax.rem(me + k, n)), device_id_type=MESH
            )
            return carry

        lax.fori_loop(1, n, greet, 0)

    kall_ref[0, z * NYH + yh] = pk_ref[0]
    kall_ref[1, yh * NZ + z] = pk_ref[1]
    hp_ref[tens] = ph_ref[...]
    hc_ref[tens] = ch_ref[...]
    lane = lax.broadcasted_iota(jnp.int32, (8, 128), 1)
    own_scores = jnp.where(
        lane == 2 * cand, sc_ref[0, 0], jnp.where(lane == 2 * cand + 1, sc_ref[0, 1], 0.0)
    )
    s1_ref[yh] = own_scores
    for c in range(2):
        for r in range(4):
            base = c * 512 + r * 128
            qs_ref[base:base + 128, :] = q_ref[c, :, r * 128:(r + 1) * 128]
    dvp_ref[...] = jnp.zeros_like(dvp_ref)
    dvc_ref[...] = jnp.zeros_like(dvc_ref)
    dkp_ref[...] = jnp.zeros_like(dkp_ref)
    dkc_ref[...] = jnp.zeros_like(dkc_ref)

    pl.semaphore_wait(barrier, (NT - 1) + (NZ - 1) + (NY - 1))

    def gather(own, whole, sems):
        a1 = Exchange(NYH, yh, at_yh, lambda p: own.at[0],
                      lambda s: whole.at[0, z * NYH + s], sems.at[0])
        b1 = Exchange(NZ, z, at_z, lambda p: own.at[1],
                      lambda s: whole.at[1, yh * NZ + s], sems.at[1])
        a2 = Exchange(NZ, z, at_z, lambda p: whole.at[0, pl.ds(z * NYH, NYH)],
                      lambda s: whole.at[0, pl.ds(s * NYH, NYH)], sems.at[2])
        b2 = Exchange(NYH, yh, at_yh, lambda p: whole.at[1, pl.ds(yh * NZ, NZ)],
                      lambda s: whole.at[1, pl.ds(s * NZ, NZ)], sems.at[3])
        return a1, b1, a2, b2

    hp_x = Exchange(NT, tens, at_t, lambda p: ph_ref, lambda s: hp_ref.at[s], sem_hp)
    hc_x = Exchange(NX, x, at_x, lambda p: ch_ref, lambda s: hc_ref.at[s * 2 + core], sem_hx)
    s_1 = Exchange(NYH, yh, at_yh, lambda p: s1_ref.at[yh], lambda s: s1_ref.at[s], sem_s.at[0])
    s_2 = Exchange(NZ, z, at_z, lambda p: s2_ref.at[z], lambda s: s2_ref.at[s], sem_s.at[1])
    k_a1, k_b1, k_a2, k_b2 = gather(pk_ref, kall_ref, sem_k)

    def sibling(xx, mine):
        slot = xx * 2 + (core if mine else other)
        return pltpu.make_async_remote_copy(
            src_ref=hc_ref.at[xx * 2 + core],
            dst_ref=hc_ref.at[slot],
            send_sem=sem_hs.at[0, xx],
            recv_sem=sem_hs.at[1, xx],
            device_id=(dp, cand, x * 2 + other),
            device_id_type=MESH,
        )

    hp_x.start()
    s_1.start()
    k_a1.start()
    k_b1.start()
    hc_x.start()
    sibling(x, True).start()

    s_1.wait_recv()
    s2_ref[z] = s1_ref[0] + s1_ref[1] + s1_ref[2] + s1_ref[3]
    s_2.start()
    k_a1.wait_recv()
    k_a2.start()
    k_b1.wait_recv()
    k_b2.start()

    hp_x.wait_recv()
    hp_rows = hp_ref[...].reshape(256, 512)
    row_block = lax.rem(lax.broadcasted_iota(jnp.int32, (256, 128), 0), 8)
    pv = jnp.zeros((256, 128), F32)
    for b in range(8):
        part = dot(hp_rows, w_ref[b * 512:(b + 1) * 512, :])
        pv = jnp.where(row_block == b, part, pv)
    pv = jnp.sum(pv.reshape(32, 8, 128), axis=1).astype(BF16).reshape(2, 16, 128)
    vall_ref[0, z * NYH + yh] = pv[0]
    vall_ref[1, yh * NZ + z] = pv[1]

    class Own:
        def __init__(self, first, second):
            self.at = (first, second)

    v_a1, v_b1, v_a2, v_b2 = gather(
        Own(vall_ref.at[0, z * NYH + yh], vall_ref.at[1, yh * NZ + z]), vall_ref, sem_v
    )
    v_a1.start()
    v_b1.start()

    s_2.wait_recv()
    total = s2_ref[0]
    for i in range(1, NZ):
        total = total + s2_ref[i]
    list_grad = rank_gradient(total[0:1, 0:64], rk_ref[...])
    place = lax.broadcasted_iota(jnp.int32, (64, 1), 0)
    for c in range(2):
        own_grad = jnp.sum(
            jnp.where(place == 2 * cand + c, list_grad, 0.0), axis=0, keepdims=True
        )
        live = lax.broadcasted_iota(jnp.int32, (CAND, 128), 0) < ln_ref[0, c]
        for r in range(4):
            base = c * 512 + r * 128
            part = oc_ref[c, :, r * 128:(r + 1) * 128].astype(F32) * own_grad
            cs_ref[base:base + 128, :] = jnp.where(live, part, 0.0).astype(BF16)

    v_a1.wait_recv()
    v_a2.start()
    v_b1.wait_recv()
    v_b2.start()
    k_a2.wait_recv()
    k_b2.wait_recv()
    kt_ref[...] = kall_ref[...].reshape(PREFIX, HEAD).astype(F32).T.astype(BF16)

    def soft(n, carry):
        c = n // 2
        cols = pl.ds(pl.multiple_of(n * CHUNK, CHUNK), CHUNK)
        queries = qs_ref[cols, :]
        cot = cs_ref[cols, :]
        log_p = dot_nt(kall_ref[...].reshape(PREFIX, HEAD), queries) * INV_ROOT
        log_c = dot_nt(ck_ref[c], queries) * INV_ROOT
        slot = lax.broadcasted_iota(jnp.int32, (CAND, CHUNK), 0)
        position = lax.rem(lax.broadcasted_iota(jnp.int32, (CAND, CHUNK), 1), CAND)
        allowed = (slot <= position) & (slot < ln_ref[0, c])
        log_c = jnp.where(allowed, log_c, -jnp.inf)
        top = jnp.maximum(
            jnp.max(log_p, axis=0, keepdims=True), jnp.max(log_c, axis=0, keepdims=True)
        )
        exp_p = jnp.exp(log_p - top)
        exp_c = jnp.exp(log_c - top)
        inverse = 1.0 / (
            jnp.sum(exp_p, axis=0, keepdims=True) + jnp.sum(exp_c, axis=0, keepdims=True)
        )
        prob_p = exp_p * inverse
        prob_c = exp_c * inverse
        p_ref[0:PREFIX, cols] = prob_p
        p_ref[PREFIX:PREFIX + CAND, cols] = prob_c
        dvp_ref[...] += dot(prob_p.astype(BF16), cot)
        dvc_ref[c] += dot(prob_c.astype(BF16), cot)
        return carry

    lax.fori_loop(0, 4, soft, 0)

    def scatter(whole, ra1, rb1, ra2, rb2, ta2, tb2, sems, ny, my_y, at_group):
        a1 = Exchange(NZ, z, at_z, lambda p: whole.at[0, pl.ds(p * ny, ny)],
                      lambda s: ra1.at[s], sems.at[0])
        b1 = Exchange(ny, my_y, at_group, lambda p: whole.at[1, pl.ds(p * NZ, NZ)],
                      lambda s: rb1.at[s], sems.at[1])
        a2 = Exchange(ny, my_y, at_group, lambda p: ta2.at[p], lambda s: ra2.at[s], sems.at[2])
        b2 = Exchange(NZ, z, at_z, lambda p: tb2.at[p], lambda s: rb2.at[s], sems.at[3])

        def middle():
            a1.wait_recv()
            ra1[z] = whole[0, pl.ds(z * ny, ny)]
            total = ra1[0].astype(F32)
            for i in range(1, NZ):
                total = total + ra1[i].astype(F32)
            ta2[...] = total.astype(BF16)
            a2.start()
            b1.wait_recv()
            rb1[my_y] = whole[1, pl.ds(my_y * NZ, NZ)]
            total = rb1[0].astype(F32)
            for i in range(1, ny):
                total = total + rb1[i].astype(F32)
            tb2[...] = total.astype(BF16)
            b2.start()

        def end():
            a2.wait_recv()
            ra2[my_y] = ta2[my_y]
            first = ra2[0].astype(F32)
            for i in range(1, ny):
                first = first + ra2[i].astype(F32)
            b2.wait_recv()
            rb2[z] = tb2[z]
            second = rb2[0].astype(F32)
            for i in range(1, NZ):
                second = second + rb2[i].astype(F32)
            return first, second

        return (a1, b1, a2, b2), middle, end

    dv_all, dv_middle, dv_end = scatter(
        send_v, rva1, rvb1, rva2, rvb2, tva2, tvb2, sem_dv, NYH, yh, at_yh
    )
    send_v[...] = dvp_ref[...].astype(BF16).reshape(2, 32, 16, HEAD)
    dv_all[0].start()
    dv_all[1].start()

    def pass_on(k, carry):
        sender = lax.rem(x + NX - k, NX)
        hc_x.copy(k, sender).wait_recv()
        sibling(sender, True).start()
        return carry

    lax.fori_loop(1, NX, pass_on, 0)

    def from_sibling(k, carry):
        sibling(k, False).wait_recv()
        return carry

    lax.fori_loop(0, NX, from_sibling, 0)

    hidden = hc_ref[...].reshape(256, WIDTH)
    cv = dot(hidden, w_ref[...]).astype(BF16).reshape(8, 2, 16, HEAD)
    for c in range(2):
        vc_ref[c] = cv[:, c].reshape(CAND, HEAD)
        dvr_ref[:, c] = dvc_ref[c].reshape(8, 16, HEAD)
    dvr_t = dvr_ref[...].reshape(256, HEAD).T.astype(BF16)

    dv_middle()
    v_a2.wait_recv()
    v_b2.wait_recv()

    def score(n, carry):
        c = n // 2
        cols = pl.ds(pl.multiple_of(n * CHUNK, CHUNK), CHUNK)
        queries = qs_ref[cols, :]
        cot = cs_ref[cols, :]
        dprob_p = dot_nt(vall_ref[...].reshape(PREFIX, HEAD), cot)
        dprob_c = dot_nt(vc_ref[c], cot)
        prob_p = p_ref[0:PREFIX, cols]
        prob_c = p_ref[PREFIX:PREFIX + CAND, cols]
        row_total = jnp.sum(prob_p * dprob_p, axis=0, keepdims=True) + jnp.sum(
            prob_c * dprob_c, axis=0, keepdims=True
        )
        ds_p = (prob_p * (dprob_p - row_total)).astype(BF16)
        ds_c = (prob_c * (dprob_c - row_total)).astype(BF16)
        dkp_ref[...] += dot(ds_p, queries)
        dkc_ref[c] += dot(ds_c, queries)
        kc_t = ck_ref[c].astype(F32).T.astype(BF16)
        gq_t = (dot(kt_ref[...], ds_p) + dot(kc_t, ds_c)) * INV_ROOT
        p_ref[0:128, cols] = gq_t
        return carry

    lax.fori_loop(0, 2, score, 0)

    first, second = dv_end()
    gpv_ref[0] = first.astype(BF16)
    gpv_ref[1] = second.astype(BF16)
    own_dv = gpv_ref[...].astype(F32).reshape(32, HEAD)
    spread = jnp.broadcast_to(own_dv[:, None, :], (32, 8, HEAD)).reshape(256, HEAD)
    spread_t = spread.T
    lane_block = lax.rem(lax.broadcasted_iota(jnp.int32, (HEAD, 256), 1), 8)

    def weight(b, carry):
        cols = pl.ds(pl.multiple_of(b * 512, 512), 512)
        own = jnp.where(lane_block == b, spread_t, 0.0).astype(BF16)
        part = dot(dvr_t, hc_ref[:, :, cols].reshape(256, 512))
        part = part + dot(own, hp_ref[...].reshape(256, 512))
        rows = part.T.astype(BF16).reshape(2, NYH, 2, 32, HEAD)
        d, zz = b // 4, lax.rem(b, 4) * 2
        for i in range(2):
            for j in range(NYH):
                send_w[0, (zz + i) * NY + d * NYH + j] = rows[i, j, 0]
                send_w[1, (d * NYH + j) * NZ + zz + i] = rows[i, j, 1]
        return carry

    lax.fori_loop(0, 8, weight, 0)
    dw_all, dw_middle, dw_end = scatter(
        send_w, rwa1, rwb1, rwa2, rwb2, twa2, twb2, sem_dw, NY, y, at_y
    )
    dw_all[0].start()
    dw_all[1].start()

    lax.fori_loop(2, 4, score, 0)

    dk_all, dk_middle, dk_end = scatter(
        send_k, rka1, rkb1, rka2, rkb2, tka2, tkb2, sem_dk, NYH, yh, at_yh
    )
    send_k[...] = (dkp_ref[...] * INV_ROOT).astype(BF16).reshape(2, 32, 16, HEAD)
    dk_all[0].start()
    dk_all[1].start()

    for c in range(2):
        gck_ref[c] = (dkc_ref[c] * INV_ROOT).astype(BF16)
        for r in range(4):
            base = c * 512 + r * 128
            gq_ref[c, :, r * 128:(r + 1) * 128] = (
                p_ref[0:128, base:base + 128].T.astype(BF16)
            )

    dk_middle()
    dw_middle()
    first, second = dk_end()
    gpk_ref[0] = first.astype(BF16)
    gpk_ref[1] = second.astype(BF16)
    first, second = dw_end()
    gw_ref[0:32, :] = first
    gw_ref[32:64, :] = second

    for group in (
        (hp_x, hc_x, s_1, s_2, k_a1, k_b1, k_a2, k_b2, v_a1, v_b1, v_a2, v_b2),
        dv_all, dw_all, dk_all,
    ):
        for one in group:
            one.wait_send()

    def sent(k, carry):
        sibling(k, True).wait_send()
        return carry

    lax.fori_loop(0, NX, sent, 0)


def shards(
    cand_query, cand_key, shared_prefix_key, cand_hidden, prefix_hidden, value_matrix,
    out_cotangent, cand_scores, ranking, lengths,
):
    vmem = pl.BlockSpec(memory_space=pltpu.VMEM)
    smem = pl.BlockSpec(memory_space=pltpu.SMEM)

    def small(count):
        return [
            pltpu.VMEM((NZ, count, 16, HEAD), BF16),
            pltpu.VMEM((count, NZ, 16, HEAD), BF16),
            pltpu.VMEM((count, 16, HEAD), BF16),
            pltpu.VMEM((NZ, 16, HEAD), BF16),
        ]

    gq, gck, gpk, gpv, gw = pl.pallas_call(
        kernel,
        out_shape=(
            jax.ShapeDtypeStruct((2, CAND, 512), BF16),
            jax.ShapeDtypeStruct((2, CAND, HEAD), BF16),
            jax.ShapeDtypeStruct((2, 16, HEAD), BF16),
            jax.ShapeDtypeStruct((2, 16, HEAD), BF16),
            jax.ShapeDtypeStruct((64, HEAD), F32),
        ),
        in_specs=[vmem] * 7 + [smem, vmem, smem],
        out_specs=(vmem,) * 5,
        scratch_shapes=[
            pltpu.VMEM((NT, 32, WIDTH), BF16),
            pltpu.VMEM((NT, 32, 512), BF16),
            pltpu.VMEM((2, 32, 16, HEAD), BF16),
            pltpu.VMEM((2, 32, 16, HEAD), BF16),
            pltpu.VMEM((HEAD, PREFIX), BF16),
            pltpu.VMEM((NYH, 8, 128), F32),
            pltpu.VMEM((NZ, 8, 128), F32),
            pltpu.VMEM((1024, HEAD), BF16),
            pltpu.VMEM((1024, HEAD), BF16),
            pltpu.VMEM((PREFIX + CAND, 1024), F32),
            pltpu.VMEM((2, CAND, HEAD), BF16),
            pltpu.VMEM((PREFIX, HEAD), F32),
            pltpu.VMEM((2, CAND, HEAD), F32),
            pltpu.VMEM((PREFIX, HEAD), F32),
            pltpu.VMEM((2, CAND, HEAD), F32),
            pltpu.VMEM((8, 2, 16, HEAD), F32),
            pltpu.VMEM((2, 32, 16, HEAD), BF16),
            pltpu.VMEM((2, 32, 16, HEAD), BF16),
            *small(NYH),
            *small(NYH),
            pltpu.VMEM((NYH, 16, HEAD), BF16),
            pltpu.VMEM((NZ, 16, HEAD), BF16),
            pltpu.VMEM((NYH, 16, HEAD), BF16),
            pltpu.VMEM((NZ, 16, HEAD), BF16),
            pltpu.VMEM((2, 64, 32, HEAD), BF16),
            pltpu.VMEM((NZ, NY, 32, HEAD), BF16),
            pltpu.VMEM((NY, NZ, 32, HEAD), BF16),
            pltpu.VMEM((NY, 32, HEAD), BF16),
            pltpu.VMEM((NZ, 32, HEAD), BF16),
            pltpu.VMEM((NY, 32, HEAD), BF16),
            pltpu.VMEM((NZ, 32, HEAD), BF16),
            pltpu.SemaphoreType.DMA((2, NT)),
            pltpu.SemaphoreType.DMA((2, NX)),
            pltpu.SemaphoreType.DMA((2, NX)),
            pltpu.SemaphoreType.DMA((2, 2, NZ)),
            pltpu.SemaphoreType.DMA((4, 2, NZ)),
            pltpu.SemaphoreType.DMA((4, 2, NZ)),
            pltpu.SemaphoreType.DMA((4, 2, NZ)),
            pltpu.SemaphoreType.DMA((4, 2, NZ)),
            pltpu.SemaphoreType.DMA((4, 2, NZ)),
        ],
        compiler_params=pltpu.CompilerParams(
            collective_id=0, has_side_effects=True, vmem_limit_bytes=48 * 1024 * 1024
        ),
    )(
        cand_query[0],
        cand_key[0],
        shared_prefix_key.reshape(2, 16, HEAD),
        cand_hidden.reshape(32, WIDTH),
        prefix_hidden.reshape(32, 512),
        value_matrix,
        out_cotangent[0],
        cand_scores,
        ranking,
        lengths,
    )
    return (
        gq[None],
        gck[None],
        gpk.reshape(1, 32, HEAD),
        gpv.reshape(1, 32, HEAD),
        gw,
    )


def solution(mesh):
    placed = (
        P("dp", "cand", None, "tensor"),
        P("dp", "cand", None, "tensor"),
        P("dp", "cand", "tensor"),
        P("dp", "cand", "tensor", None),
        P("dp", ("cand", "tensor"), None),
        P(None, "tensor"),
        P("dp", "cand", None, "tensor"),
        P("dp", "cand"),
        P("dp", None),
        P("dp", "cand"),
    )
    return jax.shard_map(
        shards,
        mesh=mesh,
        in_specs=placed,
        out_specs=(
            P("dp", "cand", None, "tensor"),
            P("dp", "cand", None, "tensor"),
            P("dp", "cand", "tensor"),
            P("dp", "cand", "tensor"),
            P(("dp", "cand"), "tensor"),
        ),
        check_vma=False,
    )
```

```python
import jax
import jax.numpy as jnp
from jax import lax
from jax.experimental import pallas as pl
from jax.experimental.pallas import tpu as pltpu
from jax.sharding import PartitionSpec as P

MESH = pl.DeviceIdType.MESH
BF16, F32 = jnp.bfloat16, jnp.float32
NZ, NYH, NY, NX, NT = 8, 4, 8, 4, 8
HEAD = 128
PREFIX = 1024
CAND = 128
CHUNK = 256
WIDTH = 4096
INV_ROOT = HEAD ** (-0.5)


def dot(a, b):
    return lax.dot_general(a, b, (((1,), (0,)), ((), ())), preferred_element_type=F32)


def dot_nt(a, b):
    return lax.dot_general(a, b, (((1,), (1,)), ((), ())), preferred_element_type=F32)


class Exchange:
    def __init__(self, n, me, device, src, dst, sems):
        self.n, self.me, self.device, self.src, self.dst, self.sems = n, me, device, src, dst, sems

    def copy(self, k, slot):
        peer = lax.rem(self.me + k, self.n)
        return pltpu.make_async_remote_copy(
            src_ref=self.src(peer),
            dst_ref=self.dst(slot),
            send_sem=self.sems.at[0, k],
            recv_sem=self.sems.at[1, k],
            device_id=self.device(peer),
            device_id_type=MESH,
        )

    def loop(self, step):
        def body(k, carry):
            step(k)
            return carry

        lax.fori_loop(1, self.n, body, 0)

    def start(self):
        self.loop(lambda k: self.copy(k, self.me).start())

    def wait_recv(self):
        self.loop(lambda k: self.copy(k, lax.rem(self.me + self.n - k, self.n)).wait_recv())

    def wait_send(self):
        self.loop(lambda k: self.copy(k, self.me).wait_send())


def rank_gradient(scores_row, ranking_row):
    n = ranking_row.shape[1]
    rows = lax.broadcasted_iota(jnp.int32, (n, n), 0)
    cols = lax.broadcasted_iota(jnp.int32, (n, n), 1)
    scores_col = jnp.sum(jnp.where(rows == cols, scores_row, 0.0), axis=1, keepdims=True)
    picker = ranking_row == rows
    ordered = jnp.sum(jnp.where(picker, scores_col, 0.0), axis=0, keepdims=True)
    later = cols >= rows
    masked = jnp.where(later, ordered, -jnp.inf)
    top = jnp.max(masked, axis=1, keepdims=True)
    weights = jnp.exp(masked - top)
    suffix = weights / jnp.sum(weights, axis=1, keepdims=True)
    by_rank = jnp.sum(suffix, axis=0, keepdims=True) - 1.0
    return jnp.sum(jnp.where(picker, by_rank, 0.0), axis=1, keepdims=True)


def kernel(
    q_hbm, ck_hbm, pk_hbm, ch_hbm, ph_hbm, w_hbm, oc_hbm, sc_ref, rk_ref, ln_ref,
    gq_hbm, gck_hbm, gpk_hbm, gpv_hbm, gw_hbm,
    gq_ref, gck_ref, gpk_ref, gpv_ref, gw_ref, store_sem,
    q_ref, ck_ref, pk_ref, ph_ref, w_ref, oc_ref, load_sem,
    phs_ref, own_hp, sxa, sxb, xa, xb, ga, gb,
    hc_ref, hp_ref, kall_ref, vall_ref, kt_ref, s1_ref, s2_ref,
    qs_ref, cs_ref, p_ref, vc_ref, dvp_ref, dvc_ref, dkp_ref, dkc_ref, dvr_ref,
    send_v, send_k, rva1, rvb1, rva2, rvb2, rka1, rkb1, rka2, rkb2, tva2, tvb2, tka2, tkb2,
    send_w, rwa1, rwb1, rwa2, rwb2, twa2, twb2,
    sem_hp, sem_hx, sem_hs, sem_s, sem_k, sem_v, sem_dv, sem_dk, sem_dw, sem_x, sem_g,
):
    dp = lax.axis_index("dp")
    cand = lax.axis_index("cand")
    tens = lax.axis_index("tensor")
    z, yh = cand // NYH, lax.rem(cand, NYH)
    y = dp * NYH + yh
    x, core = tens // 2, lax.rem(tens, 2)
    other = 1 - core

    def at_t(t):
        return (dp, cand, t)

    def at_x(xx):
        return (dp, cand, xx * 2 + core)

    def at_z(zz):
        return (dp, zz * NYH + yh, tens)

    def at_yh(yy):
        return (dp, z * NYH + yy, tens)

    def at_y(yy):
        return (yy // NYH, z * NYH + lax.rem(yy, NYH), tens)

    barrier = pltpu.get_barrier_semaphore()
    for n, me, device in ((NT, tens, at_t), (NZ, z, at_z), (NY, y, at_y)):
        def greet(k, carry, n=n, me=me, device=device):
            pl.semaphore_signal(
                barrier, inc=1, device_id=device(lax.rem(me + k, n)), device_id_type=MESH
            )
            return carry

        lax.fori_loop(1, n, greet, 0)

    loads = [
        pltpu.make_async_copy(src, dst, load_sem.at[i])
        for i, (src, dst) in enumerate((
            (pk_hbm, pk_ref), (ph_hbm, ph_ref), (ch_hbm, hc_ref.at[tens]), (q_hbm, q_ref),
            (ck_hbm, ck_ref), (w_hbm, w_ref), (oc_hbm, oc_ref),
        ))
    ]
    for load in loads:
        load.start()
    stores = [
        pltpu.make_async_copy(src, dst, store_sem.at[i])
        for i, (src, dst) in enumerate((
            (gq_ref, gq_hbm), (gck_ref, gck_hbm), (gpk_ref, gpk_hbm), (gpv_ref, gpv_hbm),
            (gw_ref, gw_hbm),
        ))
    ]

    loads[0].wait()
    kall_ref[0, z * NYH + yh] = pk_ref[0]
    kall_ref[1, yh * NZ + z] = pk_ref[1]
    loads[1].wait()
    own_rows = ph_ref[...].astype(F32)
    for b in range(4):
        phs_ref[b * 4:(b + 1) * 4, :] = own_rows[:, b * 1024:(b + 1) * 1024]
    own_hp[...] = phs_ref[...].astype(BF16)
    hp_ref[tens] = own_hp[...]
    loads[2].wait()
    loads[3].wait()
    lane = lax.broadcasted_iota(jnp.int32, (8, 128), 1)
    own_scores = jnp.where(
        lane == 2 * cand, sc_ref[0, 0], jnp.where(lane == 2 * cand + 1, sc_ref[0, 1], 0.0)
    )
    s1_ref[yh] = own_scores
    for c in range(2):
        for r in range(4):
            base = c * 512 + r * 128
            qs_ref[base:base + 128, :] = q_ref[c, :, r * 128:(r + 1) * 128]
    dvp_ref[...] = jnp.zeros_like(dvp_ref)
    dvc_ref[...] = jnp.zeros_like(dvc_ref)
    dkp_ref[...] = jnp.zeros_like(dkp_ref)
    dkc_ref[...] = jnp.zeros_like(dkc_ref)
    for load in loads[4:]:
        load.wait()

    pl.semaphore_wait(barrier, (NT - 1) + (NZ - 1) + (NY - 1))

    def gather(own, whole, sems):
        a1 = Exchange(NYH, yh, at_yh, lambda p: own.at[0],
                      lambda s: whole.at[0, z * NYH + s], sems.at[0])
        b1 = Exchange(NZ, z, at_z, lambda p: own.at[1],
                      lambda s: whole.at[1, yh * NZ + s], sems.at[1])
        a2 = Exchange(NZ, z, at_z, lambda p: whole.at[0, pl.ds(z * NYH, NYH)],
                      lambda s: whole.at[0, pl.ds(s * NYH, NYH)], sems.at[2])
        b2 = Exchange(NYH, yh, at_yh, lambda p: whole.at[1, pl.ds(yh * NZ, NZ)],
                      lambda s: whole.at[1, pl.ds(s * NZ, NZ)], sems.at[3])
        return a1, b1, a2, b2

    hp_x = Exchange(NT, tens, at_t, lambda p: own_hp, lambda s: hp_ref.at[s], sem_hp)
    hc_x = Exchange(NX, x, at_x, lambda p: hc_ref.at[tens],
                    lambda s: hc_ref.at[s * 2 + core], sem_hx)
    s_1 = Exchange(NYH, yh, at_yh, lambda p: s1_ref.at[yh], lambda s: s1_ref.at[s], sem_s.at[0])
    s_2 = Exchange(NZ, z, at_z, lambda p: s2_ref.at[z], lambda s: s2_ref.at[s], sem_s.at[1])
    k_a1, k_b1, k_a2, k_b2 = gather(pk_ref, kall_ref, sem_k)

    def sibling(xx, mine):
        slot = xx * 2 + (core if mine else other)
        return pltpu.make_async_remote_copy(
            src_ref=hc_ref.at[xx * 2 + core],
            dst_ref=hc_ref.at[slot],
            send_sem=sem_hs.at[0, xx],
            recv_sem=sem_hs.at[1, xx],
            device_id=(dp, cand, x * 2 + other),
            device_id_type=MESH,
        )

    k_a1.start()
    k_b1.start()
    s_1.start()
    hp_x.start()
    hc_x.start()
    sibling(x, True).start()

    k_a1.wait_recv()
    k_a2.start()
    k_b1.wait_recv()
    k_b2.start()
    s_1.wait_recv()
    s2_ref[z] = s1_ref[0] + s1_ref[1] + s1_ref[2] + s1_ref[3]
    s_2.start()

    hp_x.wait_recv()
    to = lax.broadcasted_iota(jnp.int32, (128, 128), 0)
    came = lax.broadcasted_iota(jnp.int32, (128, 128), 1)
    order = came == lax.rem(to // 4, 8) * 16 + (to // 32) * 4 + lax.rem(to, 4)
    hp_rows = dot(
        jnp.where(order, 1.0, 0.0).astype(BF16), hp_ref[...].reshape(128, 1024)
    ).astype(BF16)
    pv = jnp.zeros((32, HEAD), F32)
    for b in range(4):
        pv = pv + dot(hp_rows[b * 32:(b + 1) * 32], w_ref[b * 1024:(b + 1) * 1024, :])
    pv = pv.astype(BF16).reshape(2, 16, HEAD)
    vall_ref[0, z * NYH + yh] = pv[0]
    vall_ref[1, yh * NZ + z] = pv[1]

    class Own:
        def __init__(self, first, second):
            self.at = (first, second)

    v_a1, v_b1, v_a2, v_b2 = gather(
        Own(vall_ref.at[0, z * NYH + yh], vall_ref.at[1, yh * NZ + z]), vall_ref, sem_v
    )
    v_a1.start()
    v_b1.start()

    spot = lax.broadcasted_iota(jnp.int32, (1, 1024), 1)
    place = lax.rem(spot, 512)
    outer, inner, last = place // 128, lax.rem(place // 32, 4), lax.rem(spot, 32)
    wanted = jnp.where(
        spot < 512, outer * 256 + inner * 64 + last, inner * 256 + outer * 64 + 32 + last
    )
    sorted_hp = jnp.zeros((128, 1024), F32)
    for b in range(4):
        row = lax.broadcasted_iota(jnp.int32, (256, 1024), 0) + b * 256
        pick = jnp.where(row == wanted, 1.0, 0.0).astype(BF16)
        sorted_hp = sorted_hp + dot(hp_rows[:, b * 256:(b + 1) * 256], pick)
    sorted_hp = sorted_hp.astype(BF16)
    for d in range(2):
        for zh in range(2):
            rows = sorted_hp[(d * 2 + zh) * 32:(d * 2 + zh + 1) * 32]
            for j in range(4):
                sxa[zh * 4 + j, :, d * 128:(d + 1) * 128] = rows[:, j * 128:(j + 1) * 128]
                sxb[d * 4 + j, :, zh * 128:(zh + 1) * 128] = (
                    rows[:, 512 + j * 128:512 + (j + 1) * 128]
                )
    xa[z] = sxa[z]
    xb[y] = sxb[y]
    x_a = Exchange(NZ, z, at_z, lambda p: sxa.at[p], lambda s: xa.at[s], sem_x.at[0])
    x_b = Exchange(NY, y, at_y, lambda p: sxb.at[p], lambda s: xb.at[s], sem_x.at[1])
    x_a.start()
    x_b.start()

    s_2.wait_recv()
    total = s2_ref[0]
    for i in range(1, NZ):
        total = total + s2_ref[i]
    list_grad = rank_gradient(total[0:1, 0:64], rk_ref[...])
    item = lax.broadcasted_iota(jnp.int32, (64, 1), 0)
    for c in range(2):
        own_grad = jnp.sum(
            jnp.where(item == 2 * cand + c, list_grad, 0.0), axis=0, keepdims=True
        )
        live = lax.broadcasted_iota(jnp.int32, (CAND, 128), 0) < ln_ref[0, c]
        for r in range(4):
            base = c * 512 + r * 128
            part = oc_ref[c, :, r * 128:(r + 1) * 128].astype(F32) * own_grad
            cs_ref[base:base + 128, :] = jnp.where(live, part, 0.0).astype(BF16)

    k_a2.wait_recv()
    k_b2.wait_recv()
    kt_ref[...] = kall_ref[...].reshape(PREFIX, HEAD).astype(F32).T.astype(BF16)

    def soft(n, carry):
        c = n // 2
        cols = pl.ds(pl.multiple_of(n * CHUNK, CHUNK), CHUNK)
        queries = qs_ref[cols, :]
        cot = cs_ref[cols, :]
        log_p = dot_nt(kall_ref[...].reshape(PREFIX, HEAD), queries) * INV_ROOT
        log_c = dot_nt(ck_ref[c], queries) * INV_ROOT
        slot = lax.broadcasted_iota(jnp.int32, (CAND, CHUNK), 0)
        position = lax.rem(lax.broadcasted_iota(jnp.int32, (CAND, CHUNK), 1), CAND)
        allowed = (slot <= position) & (slot < ln_ref[0, c])
        log_c = jnp.where(allowed, log_c, -jnp.inf)
        top = jnp.maximum(
            jnp.max(log_p, axis=0, keepdims=True), jnp.max(log_c, axis=0, keepdims=True)
        )
        exp_p = jnp.exp(log_p - top)
        exp_c = jnp.exp(log_c - top)
        inverse = 1.0 / (
            jnp.sum(exp_p, axis=0, keepdims=True) + jnp.sum(exp_c, axis=0, keepdims=True)
        )
        prob_p = exp_p * inverse
        prob_c = exp_c * inverse
        p_ref[0:PREFIX, cols] = prob_p
        p_ref[PREFIX:PREFIX + CAND, cols] = prob_c
        dvp_ref[...] += dot(prob_p.astype(BF16), cot)
        dvc_ref[c] += dot(prob_c.astype(BF16), cot)
        return carry

    def pass_on(k, carry):
        sender = lax.rem(x + NX - k, NX)
        hc_x.copy(k, sender).wait_recv()
        sibling(sender, True).start()
        return carry

    lax.fori_loop(0, 1, soft, 0)
    v_a1.wait_recv()
    v_a2.start()
    v_b1.wait_recv()
    v_b2.start()
    lax.fori_loop(1, 3, soft, 0)
    lax.fori_loop(1, NX, pass_on, 0)
    lax.fori_loop(3, 4, soft, 0)

    def scatter(whole, ra1, rb1, ra2, rb2, ta2, tb2, sems, ny, my_y, at_group):
        a1 = Exchange(NZ, z, at_z, lambda p: whole.at[0, pl.ds(p * ny, ny)],
                      lambda s: ra1.at[s], sems.at[0])
        b1 = Exchange(ny, my_y, at_group, lambda p: whole.at[1, pl.ds(p * NZ, NZ)],
                      lambda s: rb1.at[s], sems.at[1])
        a2 = Exchange(ny, my_y, at_group, lambda p: ta2.at[p], lambda s: ra2.at[s], sems.at[2])
        b2 = Exchange(NZ, z, at_z, lambda p: tb2.at[p], lambda s: rb2.at[s], sems.at[3])

        def middle(extra=None):
            a1.wait_recv()
            ra1[z] = whole[0, pl.ds(z * ny, ny)]
            total = ra1[0].astype(F32)
            for i in range(1, NZ):
                total = total + ra1[i].astype(F32)
            if extra is not None:
                total = total + extra(0)
            ta2[...] = total.astype(BF16)
            a2.start()
            b1.wait_recv()
            rb1[my_y] = whole[1, pl.ds(my_y * NZ, NZ)]
            total = rb1[0].astype(F32)
            for i in range(1, ny):
                total = total + rb1[i].astype(F32)
            if extra is not None:
                total = total + extra(1)
            tb2[...] = total.astype(BF16)
            b2.start()

        def end():
            a2.wait_recv()
            ra2[my_y] = ta2[my_y]
            first = ra2[0].astype(F32)
            for i in range(1, ny):
                first = first + ra2[i].astype(F32)
            b2.wait_recv()
            rb2[z] = tb2[z]
            second = rb2[0].astype(F32)
            for i in range(1, NZ):
                second = second + rb2[i].astype(F32)
            return first, second

        return (a1, b1, a2, b2), middle, end

    dv_all, dv_middle, dv_end = scatter(
        send_v, rva1, rvb1, rva2, rvb2, tva2, tvb2, sem_dv, NYH, yh, at_yh
    )
    send_v[...] = dvp_ref[...].astype(BF16).reshape(2, 32, 16, HEAD)
    dv_all[0].start()
    dv_all[1].start()

    def from_sibling(k, carry):
        sibling(k, False).wait_recv()
        return carry

    lax.fori_loop(0, NX, from_sibling, 0)
    for c in range(2):
        dvr_ref[:, c] = dvc_ref[c].reshape(8, 16, HEAD)
    dvr_t = dvr_ref[...].reshape(256, HEAD).T.astype(BF16)

    def weight(b, carry):
        cols = pl.ds(pl.multiple_of(b * 512, 512), 512)
        part = dot(dvr_t, hc_ref[:, :, cols].reshape(256, 512))
        rows = part.T.astype(BF16).reshape(2, NYH, 2, 32, HEAD)
        d, zz = b // 4, lax.rem(b, 4) * 2
        for i in range(2):
            for j in range(NYH):
                send_w[0, (zz + i) * NY + d * NYH + j] = rows[i, j, 0]
                send_w[1, (d * NYH + j) * NZ + zz + i] = rows[i, j, 1]
        return carry

    lax.fori_loop(0, 8, weight, 0)
    dw_all, dw_middle, dw_end = scatter(
        send_w, rwa1, rwb1, rwa2, rwb2, twa2, twb2, sem_dw, NY, y, at_y
    )
    dw_all[0].start()
    dw_all[1].start()

    cv = dot(hc_ref[...].reshape(256, WIDTH), w_ref[...]).astype(BF16).reshape(8, 2, 16, HEAD)
    for c in range(2):
        vc_ref[c] = cv[:, c].reshape(CAND, HEAD)
    v_a2.wait_recv()
    v_b2.wait_recv()

    def score(n, carry):
        c = n // 2
        cols = pl.ds(pl.multiple_of(n * CHUNK, CHUNK), CHUNK)
        queries = qs_ref[cols, :]
        cot = cs_ref[cols, :]
        dprob_p = dot_nt(vall_ref[...].reshape(PREFIX, HEAD), cot)
        dprob_c = dot_nt(vc_ref[c], cot)
        prob_p = p_ref[0:PREFIX, cols]
        prob_c = p_ref[PREFIX:PREFIX + CAND, cols]
        row_total = jnp.sum(prob_p * dprob_p, axis=0, keepdims=True) + jnp.sum(
            prob_c * dprob_c, axis=0, keepdims=True
        )
        ds_p = (prob_p * (dprob_p - row_total)).astype(BF16)
        ds_c = (prob_c * (dprob_c - row_total)).astype(BF16)
        dkp_ref[...] += dot(ds_p, queries)
        dkc_ref[c] += dot(ds_c, queries)
        kc_t = ck_ref[c].astype(F32).T.astype(BF16)
        gq_t = (dot(kt_ref[...], ds_p) + dot(kc_t, ds_c)) * INV_ROOT
        p_ref[0:128, cols] = gq_t
        return carry

    lax.fori_loop(0, 2, score, 0)

    dv_middle()
    lax.fori_loop(2, 4, score, 0)

    dk_all, dk_middle, dk_end = scatter(
        send_k, rka1, rkb1, rka2, rkb2, tka2, tkb2, sem_dk, NYH, yh, at_yh
    )
    send_k[...] = (dkp_ref[...] * INV_ROOT).astype(BF16).reshape(2, 32, 16, HEAD)
    dk_all[0].start()
    dk_all[1].start()

    for c in range(2):
        gck_ref[c] = (dkc_ref[c] * INV_ROOT).astype(BF16)
        for r in range(4):
            base = c * 512 + r * 128
            gq_ref[c, :, r * 128:(r + 1) * 128] = (
                p_ref[0:128, base:base + 128].T.astype(BF16)
            )
    stores[0].start()
    stores[1].start()

    first, second = dv_end()
    gpv_ref[0] = first.astype(BF16)
    gpv_ref[1] = second.astype(BF16)
    stores[3].start()
    ga[z] = gpv_ref[...]
    gb[y] = gpv_ref[...]
    g_a = Exchange(NZ, z, at_z, lambda p: ga.at[z], lambda s: ga.at[s], sem_g.at[0])
    g_b = Exchange(NY, y, at_y, lambda p: gb.at[y], lambda s: gb.at[s], sem_g.at[1])
    g_a.start()
    g_b.start()
    dk_middle()
    x_a.wait_recv()
    x_b.wait_recv()

    def prefix_part(half):
        (g_a, g_b)[half].wait_recv()
        rows = (ga, gb)[half][...].reshape(256, HEAD).astype(F32).T.astype(BF16)
        part = dot(rows, (xa, xb)[half][...].reshape(256, 256))
        return part.T.reshape(8, 32, HEAD)

    dw_middle(prefix_part)
    first, second = dk_end()
    gpk_ref[0] = first.astype(BF16)
    gpk_ref[1] = second.astype(BF16)
    stores[2].start()
    first, second = dw_end()
    gw_ref[0:32, :] = first
    gw_ref[32:64, :] = second
    stores[4].start()

    for group in (
        (hp_x, hc_x, s_1, s_2, k_a1, k_b1, k_a2, k_b2, v_a1, v_b1, v_a2, v_b2,
         x_a, x_b, g_a, g_b),
        dv_all, dw_all, dk_all,
    ):
        for one in group:
            one.wait_send()

    def sent(k, carry):
        sibling(k, True).wait_send()
        return carry

    lax.fori_loop(0, NX, sent, 0)
    for store in stores:
        store.wait()


def hand_over(*refs):
    sources, results, sems = refs[:5], refs[5:10], refs[10]
    copies = [pltpu.make_async_copy(a, b, sems.at[i]) for i, (a, b) in enumerate(zip(sources, results))]
    for copy in copies:
        copy.start()
    for copy in copies:
        copy.wait()


def shards(
    cand_query, cand_key, shared_prefix_key, cand_hidden, prefix_hidden, value_matrix,
    out_cotangent, cand_scores, ranking, lengths,
):
    vmem = pl.BlockSpec(memory_space=pltpu.VMEM)
    smem = pl.BlockSpec(memory_space=pltpu.SMEM)

    def small(count):
        return [
            pltpu.VMEM((NZ, count, 16, HEAD), BF16),
            pltpu.VMEM((count, NZ, 16, HEAD), BF16),
            pltpu.VMEM((count, 16, HEAD), BF16),
            pltpu.VMEM((NZ, 16, HEAD), BF16),
        ]

    hbm = pl.BlockSpec(memory_space=pltpu.HBM)
    shapes = (
        jax.ShapeDtypeStruct((2, CAND, 512), BF16),
        jax.ShapeDtypeStruct((2, CAND, HEAD), BF16),
        jax.ShapeDtypeStruct((2, 16, HEAD), BF16),
        jax.ShapeDtypeStruct((2, 16, HEAD), BF16),
        jax.ShapeDtypeStruct((64, HEAD), F32),
    )
    results = pl.pallas_call(
        kernel,
        out_shape=shapes,
        in_specs=[hbm] * 7 + [smem, vmem, smem],
        out_specs=(hbm,) * 5,
        scratch_shapes=[
            *(pltpu.VMEM(one.shape, one.dtype) for one in shapes),
            pltpu.SemaphoreType.DMA((5,)),
            pltpu.VMEM((2, CAND, 512), BF16),
            pltpu.VMEM((2, CAND, HEAD), BF16),
            pltpu.VMEM((2, 16, HEAD), BF16),
            pltpu.VMEM((4, WIDTH), BF16),
            pltpu.VMEM((WIDTH, HEAD), BF16),
            pltpu.VMEM((2, CAND, 512), BF16),
            pltpu.SemaphoreType.DMA((7,)),
            pltpu.VMEM((16, 1024), F32),
            pltpu.VMEM((16, 1024), BF16),
            pltpu.VMEM((NZ, 32, 256), BF16),
            pltpu.VMEM((NY, 32, 256), BF16),
            pltpu.VMEM((NZ, 32, 256), BF16),
            pltpu.VMEM((NY, 32, 256), BF16),
            pltpu.VMEM((NZ, 2, 16, HEAD), BF16),
            pltpu.VMEM((NY, 2, 16, HEAD), BF16),
            pltpu.VMEM((NT, 32, WIDTH), BF16),
            pltpu.VMEM((NT, 16, 1024), BF16),
            pltpu.VMEM((2, 32, 16, HEAD), BF16),
            pltpu.VMEM((2, 32, 16, HEAD), BF16),
            pltpu.VMEM((HEAD, PREFIX), BF16),
            pltpu.VMEM((NYH, 8, 128), F32),
            pltpu.VMEM((NZ, 8, 128), F32),
            pltpu.VMEM((1024, HEAD), BF16),
            pltpu.VMEM((1024, HEAD), BF16),
            pltpu.VMEM((PREFIX + CAND, 1024), F32),
            pltpu.VMEM((2, CAND, HEAD), BF16),
            pltpu.VMEM((PREFIX, HEAD), F32),
            pltpu.VMEM((2, CAND, HEAD), F32),
            pltpu.VMEM((PREFIX, HEAD), F32),
            pltpu.VMEM((2, CAND, HEAD), F32),
            pltpu.VMEM((8, 2, 16, HEAD), F32),
            pltpu.VMEM((2, 32, 16, HEAD), BF16),
            pltpu.VMEM((2, 32, 16, HEAD), BF16),
            *small(NYH),
            *small(NYH),
            pltpu.VMEM((NYH, 16, HEAD), BF16),
            pltpu.VMEM((NZ, 16, HEAD), BF16),
            pltpu.VMEM((NYH, 16, HEAD), BF16),
            pltpu.VMEM((NZ, 16, HEAD), BF16),
            pltpu.VMEM((2, 64, 32, HEAD), BF16),
            pltpu.VMEM((NZ, NY, 32, HEAD), BF16),
            pltpu.VMEM((NY, NZ, 32, HEAD), BF16),
            pltpu.VMEM((NY, 32, HEAD), BF16),
            pltpu.VMEM((NZ, 32, HEAD), BF16),
            pltpu.VMEM((NY, 32, HEAD), BF16),
            pltpu.VMEM((NZ, 32, HEAD), BF16),
            pltpu.SemaphoreType.DMA((2, NT)),
            pltpu.SemaphoreType.DMA((2, NX)),
            pltpu.SemaphoreType.DMA((2, NX)),
            pltpu.SemaphoreType.DMA((2, 2, NZ)),
            pltpu.SemaphoreType.DMA((4, 2, NZ)),
            pltpu.SemaphoreType.DMA((4, 2, NZ)),
            pltpu.SemaphoreType.DMA((4, 2, NZ)),
            pltpu.SemaphoreType.DMA((4, 2, NZ)),
            pltpu.SemaphoreType.DMA((4, 2, NZ)),
            pltpu.SemaphoreType.DMA((2, 2, NZ)),
            pltpu.SemaphoreType.DMA((2, 2, NZ)),
        ],
        compiler_params=pltpu.CompilerParams(
            collective_id=0, has_side_effects=True, vmem_limit_bytes=64 * 1024 * 1024
        ),
    )(
        cand_query[0],
        cand_key[0],
        shared_prefix_key.reshape(2, 16, HEAD),
        cand_hidden.reshape(32, WIDTH),
        prefix_hidden[0],
        value_matrix,
        out_cotangent[0],
        cand_scores,
        ranking,
        lengths,
    )
    gq, gck, gpk, gpv, gw = pl.pallas_call(
        hand_over,
        out_shape=shapes,
        in_specs=[pl.BlockSpec(memory_space=pl.ANY)] * 5,
        out_specs=(hbm,) * 5,
        scratch_shapes=[pltpu.SemaphoreType.DMA((5,))],
    )(*results)
    return (
        gq[None],
        gck[None],
        gpk.reshape(1, 32, HEAD),
        gpv.reshape(1, 32, HEAD),
        gw,
    )


def solution(mesh):
    placed = (
        P("dp", "cand", None, "tensor"),
        P("dp", "cand", None, "tensor"),
        P("dp", "cand", "tensor"),
        P("dp", "cand", "tensor", None),
        P("dp", ("cand", "tensor"), None),
        P(None, "tensor"),
        P("dp", "cand", None, "tensor"),
        P("dp", "cand"),
        P("dp", None),
        P("dp", "cand"),
    )
    return jax.shard_map(
        shards,
        mesh=mesh,
        in_specs=placed,
        out_specs=(
            P("dp", "cand", None, "tensor"),
            P("dp", "cand", None, "tensor"),
            P("dp", "cand", "tensor"),
            P("dp", "cand", "tensor"),
            P(("dp", "cand"), "tensor"),
        ),
        check_vma=False,
    )
```

```python
import jax
import jax.numpy as jnp
from jax import lax
from jax.experimental import pallas as pl
from jax.experimental.pallas import tpu as pltpu
from jax.sharding import PartitionSpec as P

MESH = pl.DeviceIdType.MESH
BF16, F32 = jnp.bfloat16, jnp.float32
NZ, NYH, NY, NX, NT = 8, 4, 8, 4, 8
HEAD = 128
PREFIX = 1024
CAND = 128
CHUNK = 256
WIDTH = 4096
INV_ROOT = HEAD ** (-0.5)
EXP_SCALE = INV_ROOT * 1.4426950408889634


def dot(a, b):
    return lax.dot_general(a, b, (((1,), (0,)), ((), ())), preferred_element_type=F32)


def dot_nt(a, b):
    return lax.dot_general(a, b, (((1,), (1,)), ((), ())), preferred_element_type=F32)


class Exchange:
    def __init__(self, n, me, device, src, dst, sems):
        self.n, self.me, self.device, self.src, self.dst, self.sems = n, me, device, src, dst, sems

    def copy(self, k, slot):
        peer = lax.rem(self.me + k, self.n)
        return pltpu.make_async_remote_copy(
            src_ref=self.src(peer),
            dst_ref=self.dst(slot),
            send_sem=self.sems.at[0, k],
            recv_sem=self.sems.at[1, k],
            device_id=self.device(peer),
            device_id_type=MESH,
        )

    def loop(self, step):
        def body(i, carry):
            step(self.n // 2 + (i + 1) // 2 * (1 - 2 * lax.rem(i, 2)))
            return carry

        lax.fori_loop(0, self.n - 1, body, 0)

    def start(self):
        self.loop(lambda k: self.copy(k, self.me).start())

    def wait_recv(self):
        self.loop(lambda k: self.copy(k, lax.rem(self.me + self.n - k, self.n)).wait_recv())

    def wait_send(self):
        self.loop(lambda k: self.copy(k, self.me).wait_send())


def rank_gradient(scores_row, ranking_row):
    n = ranking_row.shape[1]
    rows = lax.broadcasted_iota(jnp.int32, (n, n), 0)
    cols = lax.broadcasted_iota(jnp.int32, (n, n), 1)
    scores_col = jnp.sum(jnp.where(rows == cols, scores_row, 0.0), axis=1, keepdims=True)
    picker = ranking_row == rows
    ordered = jnp.sum(jnp.where(picker, scores_col, 0.0), axis=0, keepdims=True)
    later = cols >= rows
    masked = jnp.where(later, ordered, -jnp.inf)
    top = jnp.max(masked, axis=1, keepdims=True)
    weights = jnp.exp(masked - top)
    suffix = weights / jnp.sum(weights, axis=1, keepdims=True)
    by_rank = jnp.sum(suffix, axis=0, keepdims=True) - 1.0
    return jnp.sum(jnp.where(picker, by_rank, 0.0), axis=1, keepdims=True)


def kernel(
    q_hbm, ck_hbm, pk_hbm, ch_hbm, ph_hbm, w_hbm, oc_hbm, sc_ref, rk_ref, ln_ref,
    gq_hbm, gck_hbm, gpk_hbm, gpv_hbm, gw_hbm,
    gq_ref, gck_ref, gpk_ref, gpv_ref, gw_ref, store_sem,
    q_ref, ck_ref, pk_ref, ph_ref, w_ref, oc_ref, load_sem,
    phs_ref, own_hp, sxa, sxb, xa, xb, ga, gb,
    hc_ref, hp_ref, kall_ref, vall_ref, kt_ref, s1_ref, s2_ref,
    qs_ref, cs_ref, p_ref, inv_ref, vc_ref, dvp_ref, dvc_ref, dkp_ref, dkc_ref, dvr_ref,
    send_v, send_k, rva1, rvb1, rva2, rvb2, rka1, rkb1, rka2, rkb2, tva2, tvb2, tka2, tkb2,
    send_w, rwa1, rwb1, rwa2, rwb2, twa2, twb2,
    sem_hp, sem_hx, sem_hs, sem_s, sem_k, sem_v, sem_dv, sem_dk, sem_dw, sem_x, sem_g,
):
    dp = lax.axis_index("dp")
    cand = lax.axis_index("cand")
    tens = lax.axis_index("tensor")
    z, yh = cand // NYH, lax.rem(cand, NYH)
    y = yh * 2 + dp
    x, core = tens // 2, lax.rem(tens, 2)
    other = 1 - core

    def at_t(t):
        return (dp, cand, t)

    def at_x(xx):
        return (dp, cand, xx * 2 + core)

    def at_z(zz):
        return (dp, zz * NYH + yh, tens)

    def at_yh(yy):
        return (dp, z * NYH + yy, tens)

    def at_y(yy):
        return (lax.rem(yy, 2), z * NYH + yy // 2, tens)

    barrier = pltpu.get_barrier_semaphore()
    for n, me, device in ((NT, tens, at_t), (NZ, z, at_z), (NY, y, at_y)):
        def greet(k, carry, n=n, me=me, device=device):
            pl.semaphore_signal(
                barrier, inc=1, device_id=device(lax.rem(me + k, n)), device_id_type=MESH
            )
            return carry

        lax.fori_loop(1, n, greet, 0)

    loads = [
        pltpu.make_async_copy(src, dst, load_sem.at[i])
        for i, (src, dst) in enumerate((
            (pk_hbm, pk_ref), (ph_hbm, ph_ref), (ch_hbm, hc_ref.at[tens]), (q_hbm, q_ref),
            (ck_hbm, ck_ref), (w_hbm, w_ref), (oc_hbm, oc_ref),
        ))
    ]
    for load in loads:
        load.start()
    stores = [
        pltpu.make_async_copy(src, dst, store_sem.at[i])
        for i, (src, dst) in enumerate((
            (gq_ref, gq_hbm), (gck_ref, gck_hbm), (gpk_ref, gpk_hbm), (gpv_ref, gpv_hbm),
            (gw_ref, gw_hbm),
        ))
    ]

    loads[0].wait()
    kall_ref[0, z * NYH + yh] = pk_ref[0]
    kall_ref[1, yh * NZ + z] = pk_ref[1]
    loads[1].wait()
    own_rows = ph_ref[...].astype(F32)
    for b in range(4):
        phs_ref[b * 4:(b + 1) * 4, :] = own_rows[:, b * 1024:(b + 1) * 1024]
    own_hp[...] = phs_ref[...].astype(BF16)
    hp_ref[tens] = own_hp[...]
    loads[2].wait()
    loads[3].wait()
    lane = lax.broadcasted_iota(jnp.int32, (8, 128), 1)
    own_scores = jnp.where(
        lane == 2 * cand, sc_ref[0, 0], jnp.where(lane == 2 * cand + 1, sc_ref[0, 1], 0.0)
    )
    s1_ref[yh] = own_scores
    for c in range(2):
        for r in range(4):
            base = c * 512 + r * 128
            qs_ref[base:base + 128, :] = q_ref[c, :, r * 128:(r + 1) * 128]
    dvp_ref[...] = jnp.zeros_like(dvp_ref)
    dvc_ref[...] = jnp.zeros_like(dvc_ref)
    dkp_ref[...] = jnp.zeros_like(dkp_ref)
    dkc_ref[...] = jnp.zeros_like(dkc_ref)
    for load in loads[4:]:
        load.wait()

    pl.semaphore_wait(barrier, (NT - 1) + (NZ - 1) + (NY - 1))

    def gather(own, whole, sems):
        a1 = Exchange(NYH, yh, at_yh, lambda p: own.at[0],
                      lambda s: whole.at[0, z * NYH + s], sems.at[0])
        b1 = Exchange(NZ, z, at_z, lambda p: own.at[1],
                      lambda s: whole.at[1, yh * NZ + s], sems.at[1])
        a2 = Exchange(NZ, z, at_z, lambda p: whole.at[0, pl.ds(z * NYH, NYH)],
                      lambda s: whole.at[0, pl.ds(s * NYH, NYH)], sems.at[2])
        b2 = Exchange(NYH, yh, at_yh, lambda p: whole.at[1, pl.ds(yh * NZ, NZ)],
                      lambda s: whole.at[1, pl.ds(s * NZ, NZ)], sems.at[3])
        return a1, b1, a2, b2

    hp_x = Exchange(NT, tens, at_t, lambda p: own_hp, lambda s: hp_ref.at[s], sem_hp)
    hc_x = Exchange(NX, x, at_x, lambda p: hc_ref.at[tens],
                    lambda s: hc_ref.at[s * 2 + core], sem_hx)
    s_1 = Exchange(NYH, yh, at_yh, lambda p: s1_ref.at[yh], lambda s: s1_ref.at[s], sem_s.at[0])
    s_2 = Exchange(NZ, z, at_z, lambda p: s2_ref.at[z], lambda s: s2_ref.at[s], sem_s.at[1])
    k_a1, k_b1, k_a2, k_b2 = gather(pk_ref, kall_ref, sem_k)

    def sibling(xx, mine):
        slot = xx * 2 + (core if mine else other)
        return pltpu.make_async_remote_copy(
            src_ref=hc_ref.at[xx * 2 + core],
            dst_ref=hc_ref.at[slot],
            send_sem=sem_hs.at[0, xx],
            recv_sem=sem_hs.at[1, xx],
            device_id=(dp, cand, x * 2 + other),
            device_id_type=MESH,
        )

    k_a1.start()
    k_b1.start()
    s_1.start()
    hp_x.start()
    hc_x.start()
    sibling(x, True).start()

    k_a1.wait_recv()
    k_a2.start()
    k_b1.wait_recv()
    k_b2.start()
    s_1.wait_recv()
    s2_ref[z] = s1_ref[0] + s1_ref[1] + s1_ref[2] + s1_ref[3]
    s_2.start()

    hp_x.wait_recv()
    to = lax.broadcasted_iota(jnp.int32, (128, 128), 0)
    came = lax.broadcasted_iota(jnp.int32, (128, 128), 1)
    order = came == lax.rem(to // 4, 8) * 16 + (to // 32) * 4 + lax.rem(to, 4)
    hp_rows = dot(
        jnp.where(order, 1.0, 0.0).astype(BF16), hp_ref[...].reshape(128, 1024)
    ).astype(BF16)
    pv = jnp.zeros((32, HEAD), F32)
    for b in range(4):
        pv = pv + dot(hp_rows[b * 32:(b + 1) * 32], w_ref[b * 1024:(b + 1) * 1024, :])
    pv = pv.astype(BF16).reshape(2, 16, HEAD)
    vall_ref[0, z * NYH + yh] = pv[0]
    vall_ref[1, yh * NZ + z] = pv[1]

    class Own:
        def __init__(self, first, second):
            self.at = (first, second)

    v_a1, v_b1, v_a2, v_b2 = gather(
        Own(vall_ref.at[0, z * NYH + yh], vall_ref.at[1, yh * NZ + z]), vall_ref, sem_v
    )
    v_a1.start()
    v_b1.start()

    spot = lax.broadcasted_iota(jnp.int32, (1, 1024), 1)
    place = lax.rem(spot, 512)
    outer, inner, last = place // 128, lax.rem(place // 32, 4), lax.rem(spot, 32)
    wanted = jnp.where(
        spot < 512, outer * 256 + inner * 64 + last, inner * 256 + outer * 64 + 32 + last
    )
    sorted_hp = jnp.zeros((128, 1024), F32)
    for b in range(4):
        row = lax.broadcasted_iota(jnp.int32, (256, 1024), 0) + b * 256
        pick = jnp.where(row == wanted, 1.0, 0.0).astype(BF16)
        sorted_hp = sorted_hp + dot(hp_rows[:, b * 256:(b + 1) * 256], pick)
    sorted_hp = sorted_hp.astype(BF16)
    for d in range(2):
        for zh in range(2):
            rows = sorted_hp[(d * 2 + zh) * 32:(d * 2 + zh + 1) * 32]
            for j in range(4):
                sxa[zh * 4 + j, :, d * 128:(d + 1) * 128] = rows[:, j * 128:(j + 1) * 128]
                sxb[j * 2 + d, :, zh * 128:(zh + 1) * 128] = (
                    rows[:, 512 + j * 128:512 + (j + 1) * 128]
                )
    xa[z] = sxa[z]
    xb[y] = sxb[y]
    x_a = Exchange(NZ, z, at_z, lambda p: sxa.at[p], lambda s: xa.at[s], sem_x.at[0])
    x_b = Exchange(NY, y, at_y, lambda p: sxb.at[p], lambda s: xb.at[s], sem_x.at[1])
    x_a.start()
    x_b.start()

    s_2.wait_recv()
    total = s2_ref[0]
    for i in range(1, NZ):
        total = total + s2_ref[i]
    list_grad = rank_gradient(total[0:1, 0:64], rk_ref[...])
    item = lax.broadcasted_iota(jnp.int32, (64, 1), 0)
    for c in range(2):
        own_grad = jnp.sum(
            jnp.where(item == 2 * cand + c, list_grad, 0.0), axis=0, keepdims=True
        )
        live = lax.broadcasted_iota(jnp.int32, (CAND, 128), 0) < ln_ref[0, c]
        for r in range(4):
            base = c * 512 + r * 128
            part = oc_ref[c, :, r * 128:(r + 1) * 128].astype(F32) * own_grad
            cs_ref[base:base + 128, :] = jnp.where(live, part, 0.0).astype(BF16)

    k_a2.wait_recv()
    k_b2.wait_recv()
    kt_ref[...] = kall_ref[...].reshape(PREFIX, HEAD).astype(F32).T.astype(BF16)

    def soft(n, carry):
        c = n // 2
        cols = pl.ds(pl.multiple_of(n * CHUNK, CHUNK), CHUNK)
        queries = qs_ref[cols, :]
        log_p = dot_nt(kall_ref[...].reshape(PREFIX, HEAD), queries)
        log_c = dot_nt(ck_ref[c], queries)
        slot = lax.broadcasted_iota(jnp.int32, (CAND, CHUNK), 0)
        position = lax.rem(lax.broadcasted_iota(jnp.int32, (CAND, CHUNK), 1), CAND)
        allowed = (slot <= position) & (slot < ln_ref[0, c])
        log_c = jnp.where(allowed, log_c, -jnp.inf)
        top = jnp.maximum(
            jnp.max(log_p, axis=0, keepdims=True), jnp.max(log_c, axis=0, keepdims=True)
        )
        exp_p = jnp.exp2((log_p - top) * EXP_SCALE)
        exp_c = jnp.exp2((log_c - top) * EXP_SCALE)
        inverse = 1.0 / (
            jnp.sum(exp_p, axis=0, keepdims=True) + jnp.sum(exp_c, axis=0, keepdims=True)
        )
        inv_ref[:, cols] = jnp.broadcast_to(inverse, (8, CHUNK))
        cot = (cs_ref[cols, :].astype(F32) * inverse.T).astype(BF16)
        cs_ref[cols, :] = cot
        p_ref[0:PREFIX, cols] = exp_p
        p_ref[PREFIX:PREFIX + CAND, cols] = exp_c
        dvp_ref[...] += dot(exp_p.astype(BF16), cot)
        dvc_ref[c] += dot(exp_c.astype(BF16), cot)
        return carry

    def pass_on(k, carry):
        sender = lax.rem(x + NX - k, NX)
        hc_x.copy(k, sender).wait_recv()
        sibling(sender, True).start()
        return carry

    lax.fori_loop(0, 1, soft, 0)
    v_a1.wait_recv()
    v_a2.start()
    v_b1.wait_recv()
    v_b2.start()
    lax.fori_loop(1, 3, soft, 0)
    lax.fori_loop(1, NX, pass_on, 0)
    lax.fori_loop(3, 4, soft, 0)

    def scatter(whole, ra1, rb1, ra2, rb2, ta2, tb2, sems, ny, my_y, at_group):
        a1 = Exchange(NZ, z, at_z, lambda p: whole.at[0, pl.ds(p * ny, ny)],
                      lambda s: ra1.at[s], sems.at[0])
        b1 = Exchange(ny, my_y, at_group, lambda p: whole.at[1, pl.ds(p * NZ, NZ)],
                      lambda s: rb1.at[s], sems.at[1])
        a2 = Exchange(ny, my_y, at_group, lambda p: ta2.at[p], lambda s: ra2.at[s], sems.at[2])
        b2 = Exchange(NZ, z, at_z, lambda p: tb2.at[p], lambda s: rb2.at[s], sems.at[3])

        def middle(extra=None):
            a1.wait_recv()
            ra1[z] = whole[0, pl.ds(z * ny, ny)]
            total = ra1[0].astype(F32)
            for i in range(1, NZ):
                total = total + ra1[i].astype(F32)
            if extra is not None:
                total = total + extra(0)
            ta2[...] = total.astype(BF16)
            a2.start()
            b1.wait_recv()
            rb1[my_y] = whole[1, pl.ds(my_y * NZ, NZ)]
            total = rb1[0].astype(F32)
            for i in range(1, ny):
                total = total + rb1[i].astype(F32)
            if extra is not None:
                total = total + extra(1)
            tb2[...] = total.astype(BF16)
            b2.start()

        def end():
            a2.wait_recv()
            ra2[my_y] = ta2[my_y]
            first = ra2[0].astype(F32)
            for i in range(1, ny):
                first = first + ra2[i].astype(F32)
            b2.wait_recv()
            rb2[z] = tb2[z]
            second = rb2[0].astype(F32)
            for i in range(1, NZ):
                second = second + rb2[i].astype(F32)
            return first, second

        return (a1, b1, a2, b2), middle, end

    dv_all, dv_middle, dv_end = scatter(
        send_v, rva1, rvb1, rva2, rvb2, tva2, tvb2, sem_dv, NYH, yh, at_yh
    )
    send_v[...] = dvp_ref[...].astype(BF16).reshape(2, 32, 16, HEAD)
    dv_all[0].start()
    dv_all[1].start()

    def from_sibling(k, carry):
        sibling(k, False).wait_recv()
        return carry

    lax.fori_loop(0, NX, from_sibling, 0)
    for c in range(2):
        dvr_ref[:, c] = dvc_ref[c].reshape(8, 16, HEAD)
    dvr_t = dvr_ref[...].reshape(256, HEAD).T.astype(BF16)

    def weight(b, carry):
        cols = pl.ds(pl.multiple_of(b * 512, 512), 512)
        part = dot(dvr_t, hc_ref[:, :, cols].reshape(256, 512))
        rows = part.T.astype(BF16).reshape(2, NYH, 2, 32, HEAD)
        d, zz = b // 4, lax.rem(b, 4) * 2
        for i in range(2):
            for j in range(NYH):
                send_w[0, (zz + i) * NY + j * 2 + d] = rows[i, j, 0]
                send_w[1, (j * 2 + d) * NZ + zz + i] = rows[i, j, 1]
        return carry

    lax.fori_loop(0, 8, weight, 0)
    dw_all, dw_middle, dw_end = scatter(
        send_w, rwa1, rwb1, rwa2, rwb2, twa2, twb2, sem_dw, NY, y, at_y
    )
    dw_all[0].start()
    dw_all[1].start()

    cv = dot(hc_ref[...].reshape(256, WIDTH), w_ref[...]).astype(BF16).reshape(8, 2, 16, HEAD)
    for c in range(2):
        vc_ref[c] = cv[:, c].reshape(CAND, HEAD)
    v_a2.wait_recv()
    v_b2.wait_recv()

    def score(n, carry):
        c = n // 2
        cols = pl.ds(pl.multiple_of(n * CHUNK, CHUNK), CHUNK)
        queries = qs_ref[cols, :]
        cot = cs_ref[cols, :]
        dprob_p = dot_nt(vall_ref[...].reshape(PREFIX, HEAD), cot)
        dprob_c = dot_nt(vc_ref[c], cot)
        prob_p = p_ref[0:PREFIX, cols]
        prob_c = p_ref[PREFIX:PREFIX + CAND, cols]
        row_total = jnp.sum(prob_p * dprob_p, axis=0, keepdims=True) + jnp.sum(
            prob_c * dprob_c, axis=0, keepdims=True
        )
        row_total = row_total * inv_ref[0:1, cols]
        ds_p = (prob_p * (dprob_p - row_total)).astype(BF16)
        ds_c = (prob_c * (dprob_c - row_total)).astype(BF16)
        dkp_ref[...] += dot(ds_p, queries)
        dkc_ref[c] += dot(ds_c, queries)
        kc_t = ck_ref[c].astype(F32).T.astype(BF16)
        gq_t = (dot(kt_ref[...], ds_p) + dot(kc_t, ds_c)) * INV_ROOT
        p_ref[0:128, cols] = gq_t
        return carry

    lax.fori_loop(0, 2, score, 0)

    dv_middle()
    lax.fori_loop(2, 4, score, 0)

    dk_all, dk_middle, dk_end = scatter(
        send_k, rka1, rkb1, rka2, rkb2, tka2, tkb2, sem_dk, NYH, yh, at_yh
    )
    send_k[...] = (dkp_ref[...] * INV_ROOT).astype(BF16).reshape(2, 32, 16, HEAD)
    dk_all[0].start()
    dk_all[1].start()

    for c in range(2):
        gck_ref[c] = (dkc_ref[c] * INV_ROOT).astype(BF16)
        for r in range(4):
            base = c * 512 + r * 128
            gq_ref[c, :, r * 128:(r + 1) * 128] = (
                p_ref[0:128, base:base + 128].T.astype(BF16)
            )
    stores[0].start()
    stores[1].start()

    first, second = dv_end()
    gpv_ref[0] = first.astype(BF16)
    gpv_ref[1] = second.astype(BF16)
    stores[3].start()
    ga[z] = gpv_ref[...]
    gb[y] = gpv_ref[...]
    g_a = Exchange(NZ, z, at_z, lambda p: ga.at[z], lambda s: ga.at[s], sem_g.at[0])
    g_b = Exchange(NY, y, at_y, lambda p: gb.at[y], lambda s: gb.at[s], sem_g.at[1])
    g_a.start()
    g_b.start()
    dk_middle()
    x_a.wait_recv()
    x_b.wait_recv()

    def prefix_part(half):
        (g_a, g_b)[half].wait_recv()
        rows = (ga, gb)[half][...].reshape(256, HEAD).astype(F32).T.astype(BF16)
        part = dot(rows, (xa, xb)[half][...].reshape(256, 256))
        part = part.T
        if half == 0:
            part = part.reshape(2, NYH, 32, HEAD).swapaxes(0, 1)
        return part.reshape(8, 32, HEAD)

    dw_middle(prefix_part)
    first, second = dk_end()
    gpk_ref[0] = first.astype(BF16)
    gpk_ref[1] = second.astype(BF16)
    stores[2].start()
    first, second = dw_end()
    gw_ref[0:32, :] = first
    gw_ref[32:64, :] = second
    stores[4].start()

    for group in (
        (hp_x, hc_x, s_1, s_2, k_a1, k_b1, k_a2, k_b2, v_a1, v_b1, v_a2, v_b2,
         x_a, x_b, g_a, g_b),
        dv_all, dw_all, dk_all,
    ):
        for one in group:
            one.wait_send()

    def sent(k, carry):
        sibling(k, True).wait_send()
        return carry

    lax.fori_loop(0, NX, sent, 0)
    for store in stores:
        store.wait()


def hand_over(*refs):
    sources, results, held, sems = refs[:5], refs[5:10], refs[10:15], refs[15]
    loads = [pltpu.make_async_copy(a, b, sems.at[0, i]) for i, (a, b) in enumerate(zip(sources, held))]
    stores = [pltpu.make_async_copy(a, b, sems.at[1, i]) for i, (a, b) in enumerate(zip(held, results))]
    for load in loads:
        load.start()
    for load, store in zip(loads, stores):
        load.wait()
        store.start()
    for store in stores:
        store.wait()


def shards(
    cand_query, cand_key, shared_prefix_key, cand_hidden, prefix_hidden, value_matrix,
    out_cotangent, cand_scores, ranking, lengths,
):
    vmem = pl.BlockSpec(memory_space=pltpu.VMEM)
    smem = pl.BlockSpec(memory_space=pltpu.SMEM)

    def small(count):
        return [
            pltpu.VMEM((NZ, count, 16, HEAD), BF16),
            pltpu.VMEM((count, NZ, 16, HEAD), BF16),
            pltpu.VMEM((count, 16, HEAD), BF16),
            pltpu.VMEM((NZ, 16, HEAD), BF16),
        ]

    hbm = pl.BlockSpec(memory_space=pltpu.HBM)
    shapes = (
        jax.ShapeDtypeStruct((2, CAND, 512), BF16),
        jax.ShapeDtypeStruct((2, CAND, HEAD), BF16),
        jax.ShapeDtypeStruct((2, 16, HEAD), BF16),
        jax.ShapeDtypeStruct((2, 16, HEAD), BF16),
        jax.ShapeDtypeStruct((64, HEAD), F32),
    )
    results = pl.pallas_call(
        kernel,
        out_shape=shapes,
        in_specs=[hbm] * 7 + [smem, vmem, smem],
        out_specs=(hbm,) * 5,
        scratch_shapes=[
            *(pltpu.VMEM(one.shape, one.dtype) for one in shapes),
            pltpu.SemaphoreType.DMA((5,)),
            pltpu.VMEM((2, CAND, 512), BF16),
            pltpu.VMEM((2, CAND, HEAD), BF16),
            pltpu.VMEM((2, 16, HEAD), BF16),
            pltpu.VMEM((4, WIDTH), BF16),
            pltpu.VMEM((WIDTH, HEAD), BF16),
            pltpu.VMEM((2, CAND, 512), BF16),
            pltpu.SemaphoreType.DMA((7,)),
            pltpu.VMEM((16, 1024), F32),
            pltpu.VMEM((16, 1024), BF16),
            pltpu.VMEM((NZ, 32, 256), BF16),
            pltpu.VMEM((NY, 32, 256), BF16),
            pltpu.VMEM((NZ, 32, 256), BF16),
            pltpu.VMEM((NY, 32, 256), BF16),
            pltpu.VMEM((NZ, 2, 16, HEAD), BF16),
            pltpu.VMEM((NY, 2, 16, HEAD), BF16),
            pltpu.VMEM((NT, 32, WIDTH), BF16),
            pltpu.VMEM((NT, 16, 1024), BF16),
            pltpu.VMEM((2, 32, 16, HEAD), BF16),
            pltpu.VMEM((2, 32, 16, HEAD), BF16),
            pltpu.VMEM((HEAD, PREFIX), BF16),
            pltpu.VMEM((NYH, 8, 128), F32),
            pltpu.VMEM((NZ, 8, 128), F32),
            pltpu.VMEM((1024, HEAD), BF16),
            pltpu.VMEM((1024, HEAD), BF16),
            pltpu.VMEM((PREFIX + CAND, 1024), F32),
            pltpu.VMEM((8, 1024), F32),
            pltpu.VMEM((2, CAND, HEAD), BF16),
            pltpu.VMEM((PREFIX, HEAD), F32),
            pltpu.VMEM((2, CAND, HEAD), F32),
            pltpu.VMEM((PREFIX, HEAD), F32),
            pltpu.VMEM((2, CAND, HEAD), F32),
            pltpu.VMEM((8, 2, 16, HEAD), F32),
            pltpu.VMEM((2, 32, 16, HEAD), BF16),
            pltpu.VMEM((2, 32, 16, HEAD), BF16),
            *small(NYH),
            *small(NYH),
            pltpu.VMEM((NYH, 16, HEAD), BF16),
            pltpu.VMEM((NZ, 16, HEAD), BF16),
            pltpu.VMEM((NYH, 16, HEAD), BF16),
            pltpu.VMEM((NZ, 16, HEAD), BF16),
            pltpu.VMEM((2, 64, 32, HEAD), BF16),
            pltpu.VMEM((NZ, NY, 32, HEAD), BF16),
            pltpu.VMEM((NY, NZ, 32, HEAD), BF16),
            pltpu.VMEM((NY, 32, HEAD), BF16),
            pltpu.VMEM((NZ, 32, HEAD), BF16),
            pltpu.VMEM((NY, 32, HEAD), BF16),
            pltpu.VMEM((NZ, 32, HEAD), BF16),
            pltpu.SemaphoreType.DMA((2, NT)),
            pltpu.SemaphoreType.DMA((2, NX)),
            pltpu.SemaphoreType.DMA((2, NX)),
            pltpu.SemaphoreType.DMA((2, 2, NZ)),
            pltpu.SemaphoreType.DMA((4, 2, NZ)),
            pltpu.SemaphoreType.DMA((4, 2, NZ)),
            pltpu.SemaphoreType.DMA((4, 2, NZ)),
            pltpu.SemaphoreType.DMA((4, 2, NZ)),
            pltpu.SemaphoreType.DMA((4, 2, NZ)),
            pltpu.SemaphoreType.DMA((2, 2, NZ)),
            pltpu.SemaphoreType.DMA((2, 2, NZ)),
        ],
        compiler_params=pltpu.CompilerParams(
            collective_id=0, has_side_effects=True, vmem_limit_bytes=64 * 1024 * 1024
        ),
    )(
        cand_query[0],
        cand_key[0],
        shared_prefix_key.reshape(2, 16, HEAD),
        cand_hidden.reshape(32, WIDTH),
        prefix_hidden[0],
        value_matrix,
        out_cotangent[0],
        cand_scores,
        ranking,
        lengths,
    )
    gq, gck, gpk, gpv, gw = pl.pallas_call(
        hand_over,
        out_shape=shapes,
        in_specs=[pl.BlockSpec(memory_space=pl.ANY)] * 5,
        out_specs=(hbm,) * 5,
        scratch_shapes=[
            *(pltpu.VMEM(one.shape, one.dtype) for one in shapes),
            pltpu.SemaphoreType.DMA((2, 5)),
        ],
        compiler_params=pltpu.CompilerParams(vmem_limit_bytes=64 * 1024 * 1024),
    )(*results)
    return (
        gq[None],
        gck[None],
        gpk.reshape(1, 32, HEAD),
        gpv.reshape(1, 32, HEAD),
        gw,
    )


def solution(mesh):
    placed = (
        P("dp", "cand", None, "tensor"),
        P("dp", "cand", None, "tensor"),
        P("dp", "cand", "tensor"),
        P("dp", "cand", "tensor", None),
        P("dp", ("cand", "tensor"), None),
        P(None, "tensor"),
        P("dp", "cand", None, "tensor"),
        P("dp", "cand"),
        P("dp", None),
        P("dp", "cand"),
    )
    return jax.shard_map(
        shards,
        mesh=mesh,
        in_specs=placed,
        out_specs=(
            P("dp", "cand", None, "tensor"),
            P("dp", "cand", None, "tensor"),
            P("dp", "cand", "tensor"),
            P("dp", "cand", "tensor"),
            P(("dp", "cand"), "tensor"),
        ),
        check_vma=False,
    )
```

```python
import jax
import jax.numpy as jnp
from jax import lax
from jax.experimental import pallas as pl
from jax.experimental.pallas import tpu as pltpu
from jax.sharding import PartitionSpec as P

MESH = pl.DeviceIdType.MESH
BF16, F32 = jnp.bfloat16, jnp.float32
NZ, NYH, NY, NX, NT = 8, 4, 8, 4, 8
HEAD = 128
PREFIX = 1024
CAND = 128
CHUNK = 256
WIDTH = 4096
INV_ROOT = HEAD ** (-0.5)


def dot(a, b):
    return lax.dot_general(a, b, (((1,), (0,)), ((), ())), preferred_element_type=F32)


def dot_nt(a, b):
    return lax.dot_general(a, b, (((1,), (1,)), ((), ())), preferred_element_type=F32)


class Exchange:
    def __init__(self, n, me, device, src, dst, sems):
        self.n, self.me, self.device, self.src, self.dst, self.sems = n, me, device, src, dst, sems

    def copy(self, k, slot):
        peer = lax.rem(self.me + k, self.n)
        return pltpu.make_async_remote_copy(
            src_ref=self.src(peer),
            dst_ref=self.dst(slot),
            send_sem=self.sems.at[0, k],
            recv_sem=self.sems.at[1, k],
            device_id=self.device(peer),
            device_id_type=MESH,
        )

    def loop(self, step):
        def body(k, carry):
            step(k)
            return carry

        lax.fori_loop(1, self.n, body, 0)

    def start(self):
        self.loop(lambda k: self.copy(k, self.me).start())

    def wait_recv(self):
        self.loop(lambda k: self.copy(k, lax.rem(self.me + self.n - k, self.n)).wait_recv())

    def wait_send(self):
        self.loop(lambda k: self.copy(k, self.me).wait_send())


class Ring:
    def __init__(self, me, device, whole, half, third, fourth, joined, came, sems):
        self.me, self.device, self.whole, self.half = me, device, whole, half
        self.third, self.fourth, self.joined, self.came = third, fourth, joined, came

        def copy(i, src, dst, offset):
            return pltpu.make_async_remote_copy(
                src_ref=src,
                dst_ref=dst,
                send_sem=sems.at[0, i],
                recv_sem=sems.at[1, i],
                device_id=device(lax.rem(me + offset + 8, 8)),
                device_id_type=MESH,
            )

        self.first = (
            copy(0, self.block(3), third.at[0], 1),
            copy(1, self.block(-3), third.at[1], -1),
            copy(2, self.block(4, 0, 4), fourth.at[0], 2),
            copy(3, self.block(4, 4, 4), fourth.at[1], -2),
        )
        self.near = (
            copy(4, self.block(1), came.at[0], 1),
            copy(5, self.block(-1), came.at[1], -1),
        )
        self.second = (
            copy(6, joined.at[0], came.at[2], 2),
            copy(7, joined.at[1], came.at[3], -2),
        )

    def block(self, offset, start=0, count=8):
        slot = lax.rem(self.me + offset + 8, 8) * 8 + start
        return self.whole.at[self.half, pl.ds(slot, count)]

    def start(self):
        for one in self.first + self.near:
            one.start()

    def relay(self):
        for one in self.first:
            one.wait_recv()
        for side, offset in ((0, 2), (1, -2)):
            own = self.block(offset)[...].astype(F32) + self.third[side].astype(F32)
            part = slice(side * 4, side * 4 + 4)
            rest = slice(4 - side * 4, 8 - side * 4)
            self.joined[side, part] = (own[part] + self.fourth[side].astype(F32)).astype(BF16)
            self.joined[side, rest] = own[rest].astype(BF16)
            self.second[side].start()

    def total(self):
        result = self.block(0)[...].astype(F32)
        for i, one in enumerate(self.near + self.second):
            one.wait_recv()
            result = result + self.came[i].astype(F32)
        return result

    def wait_send(self):
        for one in self.first + self.near + self.second:
            one.wait_send()


def rank_gradient(scores_row, ranking_row):
    n = ranking_row.shape[1]
    rows = lax.broadcasted_iota(jnp.int32, (n, n), 0)
    cols = lax.broadcasted_iota(jnp.int32, (n, n), 1)
    scores_col = jnp.sum(jnp.where(rows == cols, scores_row, 0.0), axis=1, keepdims=True)
    picker = ranking_row == rows
    ordered = jnp.sum(jnp.where(picker, scores_col, 0.0), axis=0, keepdims=True)
    later = cols >= rows
    masked = jnp.where(later, ordered, -jnp.inf)
    top = jnp.max(masked, axis=1, keepdims=True)
    weights = jnp.exp(masked - top)
    suffix = weights / jnp.sum(weights, axis=1, keepdims=True)
    by_rank = jnp.sum(suffix, axis=0, keepdims=True) - 1.0
    return jnp.sum(jnp.where(picker, by_rank, 0.0), axis=1, keepdims=True)


def kernel(
    q_hbm, ck_hbm, pk_hbm, ch_hbm, ph_hbm, w_hbm, oc_hbm, sc_ref, rk_ref, ln_ref,
    gq_hbm, gck_hbm, gpk_hbm, gpv_hbm, gw_hbm,
    gq_ref, gck_ref, gpk_ref, gpv_ref, gw_ref, store_sem,
    q_ref, ck_ref, pk_ref, ph_ref, w_ref, oc_ref, load_sem,
    phs_ref, own_hp, sxa, sxb, xa, xb, ga, gb,
    hc_ref, hp_ref, kall_ref, vall_ref, kt_ref, s1_ref, s2_ref,
    qs_ref, cs_ref, p_ref, vc_ref, dvp_ref, dvc_ref, dkp_ref, dkc_ref, dvr_ref,
    send_v, send_k, rva1, rvb1, rva2, rvb2, rka1, rkb1, rka2, rkb2, tva2, tvb2, tka2, tkb2,
    send_w, third_a, fourth_a, joined_a, came_a, third_b, fourth_b, joined_b, came_b,
    rwa2, rwb2, twa2, twb2,
    sem_hp, sem_hx, sem_hs, sem_s, sem_k, sem_v, sem_dv, sem_dk, sem_dw, sem_r, sem_x, sem_g,
):
    dp = lax.axis_index("dp")
    cand = lax.axis_index("cand")
    tens = lax.axis_index("tensor")
    z, yh = cand // NYH, lax.rem(cand, NYH)
    y = yh * 2 + dp
    x, core = tens // 2, lax.rem(tens, 2)
    other = 1 - core

    def at_t(t):
        return (dp, cand, t)

    def at_x(xx):
        return (dp, cand, xx * 2 + core)

    def at_z(zz):
        return (dp, zz * NYH + yh, tens)

    def at_yh(yy):
        return (dp, z * NYH + yy, tens)

    def at_y(yy):
        return (lax.rem(yy, 2), z * NYH + yy // 2, tens)

    barrier = pltpu.get_barrier_semaphore()
    for n, me, device in ((NT, tens, at_t), (NZ, z, at_z), (NY, y, at_y)):
        def greet(k, carry, n=n, me=me, device=device):
            pl.semaphore_signal(
                barrier, inc=1, device_id=device(lax.rem(me + k, n)), device_id_type=MESH
            )
            return carry

        lax.fori_loop(1, n, greet, 0)

    loads = [
        pltpu.make_async_copy(src, dst, load_sem.at[i])
        for i, (src, dst) in enumerate((
            (pk_hbm, pk_ref), (ph_hbm, ph_ref), (ch_hbm, hc_ref.at[tens]), (q_hbm, q_ref),
            (ck_hbm, ck_ref), (w_hbm, w_ref), (oc_hbm, oc_ref),
        ))
    ]
    for load in loads:
        load.start()
    stores = [
        pltpu.make_async_copy(src, dst, store_sem.at[i])
        for i, (src, dst) in enumerate((
            (gq_ref, gq_hbm), (gck_ref, gck_hbm), (gpk_ref, gpk_hbm), (gpv_ref, gpv_hbm),
            (gw_ref, gw_hbm),
        ))
    ]

    loads[0].wait()
    kall_ref[0, z * NYH + yh] = pk_ref[0]
    kall_ref[1, yh * NZ + z] = pk_ref[1]
    loads[1].wait()
    own_rows = ph_ref[...].astype(F32)
    for b in range(4):
        phs_ref[b * 4:(b + 1) * 4, :] = own_rows[:, b * 1024:(b + 1) * 1024]
    own_hp[...] = phs_ref[...].astype(BF16)
    hp_ref[tens] = own_hp[...]
    loads[2].wait()
    loads[3].wait()
    lane = lax.broadcasted_iota(jnp.int32, (8, 128), 1)
    own_scores = jnp.where(
        lane == 2 * cand, sc_ref[0, 0], jnp.where(lane == 2 * cand + 1, sc_ref[0, 1], 0.0)
    )
    s1_ref[yh] = own_scores
    for c in range(2):
        for r in range(4):
            base = c * 512 + r * 128
            qs_ref[base:base + 128, :] = q_ref[c, :, r * 128:(r + 1) * 128]
    dvp_ref[...] = jnp.zeros_like(dvp_ref)
    dvc_ref[...] = jnp.zeros_like(dvc_ref)
    dkp_ref[...] = jnp.zeros_like(dkp_ref)
    dkc_ref[...] = jnp.zeros_like(dkc_ref)
    for load in loads[4:]:
        load.wait()

    pl.semaphore_wait(barrier, (NT - 1) + (NZ - 1) + (NY - 1))

    def gather(own, whole, sems):
        a1 = Exchange(NYH, yh, at_yh, lambda p: own.at[0],
                      lambda s: whole.at[0, z * NYH + s], sems.at[0])
        b1 = Exchange(NZ, z, at_z, lambda p: own.at[1],
                      lambda s: whole.at[1, yh * NZ + s], sems.at[1])
        a2 = Exchange(NZ, z, at_z, lambda p: whole.at[0, pl.ds(z * NYH, NYH)],
                      lambda s: whole.at[0, pl.ds(s * NYH, NYH)], sems.at[2])
        b2 = Exchange(NYH, yh, at_yh, lambda p: whole.at[1, pl.ds(yh * NZ, NZ)],
                      lambda s: whole.at[1, pl.ds(s * NZ, NZ)], sems.at[3])
        return a1, b1, a2, b2

    hp_x = Exchange(NT, tens, at_t, lambda p: own_hp, lambda s: hp_ref.at[s], sem_hp)
    hc_x = Exchange(NX, x, at_x, lambda p: hc_ref.at[tens],
                    lambda s: hc_ref.at[s * 2 + core], sem_hx)
    s_1 = Exchange(NYH, yh, at_yh, lambda p: s1_ref.at[yh], lambda s: s1_ref.at[s], sem_s.at[0])
    s_2 = Exchange(NZ, z, at_z, lambda p: s2_ref.at[z], lambda s: s2_ref.at[s], sem_s.at[1])
    k_a1, k_b1, k_a2, k_b2 = gather(pk_ref, kall_ref, sem_k)

    def sibling(xx, mine):
        slot = xx * 2 + (core if mine else other)
        return pltpu.make_async_remote_copy(
            src_ref=hc_ref.at[xx * 2 + core],
            dst_ref=hc_ref.at[slot],
            send_sem=sem_hs.at[0, xx],
            recv_sem=sem_hs.at[1, xx],
            device_id=(dp, cand, x * 2 + other),
            device_id_type=MESH,
        )

    k_a1.start()
    k_b1.start()
    s_1.start()
    hp_x.start()
    hc_x.start()
    sibling(x, True).start()

    k_a1.wait_recv()
    k_a2.start()
    k_b1.wait_recv()
    k_b2.start()
    s_1.wait_recv()
    s2_ref[z] = s1_ref[0] + s1_ref[1] + s1_ref[2] + s1_ref[3]
    s_2.start()

    hp_x.wait_recv()
    to = lax.broadcasted_iota(jnp.int32, (128, 128), 0)
    came = lax.broadcasted_iota(jnp.int32, (128, 128), 1)
    order = came == lax.rem(to // 4, 8) * 16 + (to // 32) * 4 + lax.rem(to, 4)
    hp_rows = dot(
        jnp.where(order, 1.0, 0.0).astype(BF16), hp_ref[...].reshape(128, 1024)
    ).astype(BF16)
    pv = jnp.zeros((32, HEAD), F32)
    for b in range(4):
        pv = pv + dot(hp_rows[b * 32:(b + 1) * 32], w_ref[b * 1024:(b + 1) * 1024, :])
    pv = pv.astype(BF16).reshape(2, 16, HEAD)
    vall_ref[0, z * NYH + yh] = pv[0]
    vall_ref[1, yh * NZ + z] = pv[1]

    class Own:
        def __init__(self, first, second):
            self.at = (first, second)

    v_a1, v_b1, v_a2, v_b2 = gather(
        Own(vall_ref.at[0, z * NYH + yh], vall_ref.at[1, yh * NZ + z]), vall_ref, sem_v
    )
    v_a1.start()
    v_b1.start()

    spot = lax.broadcasted_iota(jnp.int32, (1, 1024), 1)
    place = lax.rem(spot, 512)
    outer, inner, last = place // 128, lax.rem(place // 32, 4), lax.rem(spot, 32)
    wanted = jnp.where(
        spot < 512, outer * 256 + inner * 64 + last, inner * 256 + outer * 64 + 32 + last
    )
    sorted_hp = jnp.zeros((128, 1024), F32)
    for b in range(4):
        row = lax.broadcasted_iota(jnp.int32, (256, 1024), 0) + b * 256
        pick = jnp.where(row == wanted, 1.0, 0.0).astype(BF16)
        sorted_hp = sorted_hp + dot(hp_rows[:, b * 256:(b + 1) * 256], pick)
    sorted_hp = sorted_hp.astype(BF16)
    for d in range(2):
        for zh in range(2):
            rows = sorted_hp[(d * 2 + zh) * 32:(d * 2 + zh + 1) * 32]
            for j in range(4):
                sxa[zh * 4 + j, :, d * 128:(d + 1) * 128] = rows[:, j * 128:(j + 1) * 128]
                sxb[j * 2 + d, :, zh * 128:(zh + 1) * 128] = (
                    rows[:, 512 + j * 128:512 + (j + 1) * 128]
                )
    xa[z] = sxa[z]
    xb[y] = sxb[y]
    x_a = Exchange(NZ, z, at_z, lambda p: sxa.at[p], lambda s: xa.at[s], sem_x.at[0])
    x_b = Exchange(NY, y, at_y, lambda p: sxb.at[p], lambda s: xb.at[s], sem_x.at[1])
    x_a.start()
    x_b.start()

    s_2.wait_recv()
    total = s2_ref[0]
    for i in range(1, NZ):
        total = total + s2_ref[i]
    list_grad = rank_gradient(total[0:1, 0:64], rk_ref[...])
    item = lax.broadcasted_iota(jnp.int32, (64, 1), 0)
    for c in range(2):
        own_grad = jnp.sum(
            jnp.where(item == 2 * cand + c, list_grad, 0.0), axis=0, keepdims=True
        )
        live = lax.broadcasted_iota(jnp.int32, (CAND, 128), 0) < ln_ref[0, c]
        for r in range(4):
            base = c * 512 + r * 128
            part = oc_ref[c, :, r * 128:(r + 1) * 128].astype(F32) * own_grad
            cs_ref[base:base + 128, :] = jnp.where(live, part, 0.0).astype(BF16)

    k_a2.wait_recv()
    k_b2.wait_recv()
    kt_ref[...] = kall_ref[...].reshape(PREFIX, HEAD).astype(F32).T.astype(BF16)

    def soft(n, carry):
        c = n // 2
        cols = pl.ds(pl.multiple_of(n * CHUNK, CHUNK), CHUNK)
        queries = qs_ref[cols, :]
        cot = cs_ref[cols, :]
        log_p = dot_nt(kall_ref[...].reshape(PREFIX, HEAD), queries) * INV_ROOT
        log_c = dot_nt(ck_ref[c], queries) * INV_ROOT
        slot = lax.broadcasted_iota(jnp.int32, (CAND, CHUNK), 0)
        position = lax.rem(lax.broadcasted_iota(jnp.int32, (CAND, CHUNK), 1), CAND)
        allowed = (slot <= position) & (slot < ln_ref[0, c])
        log_c = jnp.where(allowed, log_c, -jnp.inf)
        top = jnp.maximum(
            jnp.max(log_p, axis=0, keepdims=True), jnp.max(log_c, axis=0, keepdims=True)
        )
        exp_p = jnp.exp(log_p - top)
        exp_c = jnp.exp(log_c - top)
        inverse = 1.0 / (
            jnp.sum(exp_p, axis=0, keepdims=True) + jnp.sum(exp_c, axis=0, keepdims=True)
        )
        prob_p = exp_p * inverse
        prob_c = exp_c * inverse
        p_ref[0:PREFIX, cols] = prob_p
        p_ref[PREFIX:PREFIX + CAND, cols] = prob_c
        dvp_ref[...] += dot(prob_p.astype(BF16), cot)
        dvc_ref[c] += dot(prob_c.astype(BF16), cot)
        return carry

    def pass_on(k, carry):
        sender = lax.rem(x + NX - k, NX)
        hc_x.copy(k, sender).wait_recv()
        sibling(sender, True).start()
        return carry

    lax.fori_loop(0, 1, soft, 0)
    v_a1.wait_recv()
    v_a2.start()
    v_b1.wait_recv()
    v_b2.start()
    lax.fori_loop(1, 3, soft, 0)
    lax.fori_loop(1, NX, pass_on, 0)
    lax.fori_loop(3, 4, soft, 0)

    def scatter(whole, ra1, rb1, ra2, rb2, ta2, tb2, sems, ny, my_y, at_group):
        a1 = Exchange(NZ, z, at_z, lambda p: whole.at[0, pl.ds(p * ny, ny)],
                      lambda s: ra1.at[s], sems.at[0])
        b1 = Exchange(ny, my_y, at_group, lambda p: whole.at[1, pl.ds(p * NZ, NZ)],
                      lambda s: rb1.at[s], sems.at[1])
        a2 = Exchange(ny, my_y, at_group, lambda p: ta2.at[p], lambda s: ra2.at[s], sems.at[2])
        b2 = Exchange(NZ, z, at_z, lambda p: tb2.at[p], lambda s: rb2.at[s], sems.at[3])

        def middle():
            a1.wait_recv()
            ra1[z] = whole[0, pl.ds(z * ny, ny)]
            total = ra1[0].astype(F32)
            for i in range(1, NZ):
                total = total + ra1[i].astype(F32)
            ta2[...] = total.astype(BF16)
            a2.start()
            b1.wait_recv()
            rb1[my_y] = whole[1, pl.ds(my_y * NZ, NZ)]
            total = rb1[0].astype(F32)
            for i in range(1, ny):
                total = total + rb1[i].astype(F32)
            tb2[...] = total.astype(BF16)
            b2.start()

        def end():
            a2.wait_recv()
            ra2[my_y] = ta2[my_y]
            first = ra2[0].astype(F32)
            for i in range(1, ny):
                first = first + ra2[i].astype(F32)
            b2.wait_recv()
            rb2[z] = tb2[z]
            second = rb2[0].astype(F32)
            for i in range(1, NZ):
                second = second + rb2[i].astype(F32)
            return first, second

        return (a1, b1, a2, b2), middle, end

    dv_all, dv_middle, dv_end = scatter(
        send_v, rva1, rvb1, rva2, rvb2, tva2, tvb2, sem_dv, NYH, yh, at_yh
    )
    send_v[...] = dvp_ref[...].astype(BF16).reshape(2, 32, 16, HEAD)
    dv_all[0].start()
    dv_all[1].start()

    def from_sibling(k, carry):
        sibling(k, False).wait_recv()
        return carry

    lax.fori_loop(0, NX, from_sibling, 0)
    for c in range(2):
        dvr_ref[:, c] = dvc_ref[c].reshape(8, 16, HEAD)
    dvr_t = dvr_ref[...].reshape(256, HEAD).T.astype(BF16)

    def weight(b, carry):
        cols = pl.ds(pl.multiple_of(b * 512, 512), 512)
        part = dot(dvr_t, hc_ref[:, :, cols].reshape(256, 512))
        rows = part.T.astype(BF16).reshape(2, NYH, 2, 32, HEAD)
        d, zz = b // 4, lax.rem(b, 4) * 2
        for i in range(2):
            for j in range(NYH):
                send_w[0, (zz + i) * NY + j * 2 + d] = rows[i, j, 0]
                send_w[1, (j * 2 + d) * NZ + zz + i] = rows[i, j, 1]
        return carry

    lax.fori_loop(0, 8, weight, 0)
    ring_a = Ring(z, at_z, send_w, 0, third_a, fourth_a, joined_a, came_a, sem_r.at[0])
    ring_b = Ring(y, at_y, send_w, 1, third_b, fourth_b, joined_b, came_b, sem_r.at[1])
    dw_a = Exchange(NY, y, at_y, lambda p: twa2.at[p], lambda s: rwa2.at[s], sem_dw.at[0])
    dw_b = Exchange(NZ, z, at_z, lambda p: twb2.at[p], lambda s: rwb2.at[s], sem_dw.at[1])
    dv_middle()
    ring_a.start()
    ring_b.start()

    cv = dot(hc_ref[...].reshape(256, WIDTH), w_ref[...]).astype(BF16).reshape(8, 2, 16, HEAD)
    for c in range(2):
        vc_ref[c] = cv[:, c].reshape(CAND, HEAD)
    v_a2.wait_recv()
    v_b2.wait_recv()

    def score(n, carry):
        c = n // 2
        cols = pl.ds(pl.multiple_of(n * CHUNK, CHUNK), CHUNK)
        queries = qs_ref[cols, :]
        cot = cs_ref[cols, :]
        dprob_p = dot_nt(vall_ref[...].reshape(PREFIX, HEAD), cot)
        dprob_c = dot_nt(vc_ref[c], cot)
        prob_p = p_ref[0:PREFIX, cols]
        prob_c = p_ref[PREFIX:PREFIX + CAND, cols]
        row_total = jnp.sum(prob_p * dprob_p, axis=0, keepdims=True) + jnp.sum(
            prob_c * dprob_c, axis=0, keepdims=True
        )
        ds_p = (prob_p * (dprob_p - row_total)).astype(BF16)
        ds_c = (prob_c * (dprob_c - row_total)).astype(BF16)
        dkp_ref[...] += dot(ds_p, queries)
        dkc_ref[c] += dot(ds_c, queries)
        kc_t = ck_ref[c].astype(F32).T.astype(BF16)
        gq_t = (dot(kt_ref[...], ds_p) + dot(kc_t, ds_c)) * INV_ROOT
        p_ref[0:128, cols] = gq_t
        return carry

    lax.fori_loop(0, 1, score, 0)
    ring_a.relay()
    ring_b.relay()
    lax.fori_loop(1, 2, score, 0)

    first, second = dv_end()
    gpv_ref[0] = first.astype(BF16)
    gpv_ref[1] = second.astype(BF16)
    stores[3].start()
    ga[z] = gpv_ref[...]
    gb[y] = gpv_ref[...]
    g_a = Exchange(NZ, z, at_z, lambda p: ga.at[z], lambda s: ga.at[s], sem_g.at[0])
    g_b = Exchange(NY, y, at_y, lambda p: gb.at[y], lambda s: gb.at[s], sem_g.at[1])
    g_a.start()
    g_b.start()
    lax.fori_loop(2, 4, score, 0)

    dk_all, dk_middle, dk_end = scatter(
        send_k, rka1, rkb1, rka2, rkb2, tka2, tkb2, sem_dk, NYH, yh, at_yh
    )
    send_k[...] = (dkp_ref[...] * INV_ROOT).astype(BF16).reshape(2, 32, 16, HEAD)
    dk_all[0].start()
    dk_all[1].start()

    for c in range(2):
        gck_ref[c] = (dkc_ref[c] * INV_ROOT).astype(BF16)
        for r in range(4):
            base = c * 512 + r * 128
            gq_ref[c, :, r * 128:(r + 1) * 128] = (
                p_ref[0:128, base:base + 128].T.astype(BF16)
            )
    stores[0].start()
    stores[1].start()

    x_a.wait_recv()
    x_b.wait_recv()

    def prefix_part(half):
        (g_a, g_b)[half].wait_recv()
        rows = (ga, gb)[half][...].reshape(256, HEAD).astype(F32).T.astype(BF16)
        part = dot(rows, (xa, xb)[half][...].reshape(256, 256))
        part = part.T
        if half == 0:
            part = part.reshape(2, NYH, 32, HEAD).swapaxes(0, 1)
        return part.reshape(8, 32, HEAD)

    twa2[...] = (ring_a.total() + prefix_part(0)).astype(BF16)
    dw_a.start()
    twb2[...] = (ring_b.total() + prefix_part(1)).astype(BF16)
    dw_b.start()
    dk_middle()
    first, second = dk_end()
    gpk_ref[0] = first.astype(BF16)
    gpk_ref[1] = second.astype(BF16)
    stores[2].start()
    for i, (one, mine, sent, came) in enumerate(((dw_a, y, twa2, rwa2), (dw_b, z, twb2, rwb2))):
        one.wait_recv()
        came[mine] = sent[mine]
        last = came[0].astype(F32)
        for j in range(1, 8):
            last = last + came[j].astype(F32)
        gw_ref[i * 32:(i + 1) * 32, :] = last
    stores[4].start()

    for group in (
        (hp_x, hc_x, s_1, s_2, k_a1, k_b1, k_a2, k_b2, v_a1, v_b1, v_a2, v_b2,
         x_a, x_b, g_a, g_b),
        (ring_a, ring_b, dw_a, dw_b), dv_all, dk_all,
    ):
        for one in group:
            one.wait_send()

    def sent(k, carry):
        sibling(k, True).wait_send()
        return carry

    lax.fori_loop(0, NX, sent, 0)
    for store in stores:
        store.wait()


def hand_over(*refs):
    sources, results, held, sems = refs[:5], refs[5:10], refs[10:15], refs[15]
    loads = [pltpu.make_async_copy(a, b, sems.at[0, i]) for i, (a, b) in enumerate(zip(sources, held))]
    stores = [pltpu.make_async_copy(a, b, sems.at[1, i]) for i, (a, b) in enumerate(zip(held, results))]
    for load in loads:
        load.start()
    for load, store in zip(loads, stores):
        load.wait()
        store.start()
    for store in stores:
        store.wait()


def shards(
    cand_query, cand_key, shared_prefix_key, cand_hidden, prefix_hidden, value_matrix,
    out_cotangent, cand_scores, ranking, lengths,
):
    vmem = pl.BlockSpec(memory_space=pltpu.VMEM)
    smem = pl.BlockSpec(memory_space=pltpu.SMEM)

    def small(count):
        return [
            pltpu.VMEM((NZ, count, 16, HEAD), BF16),
            pltpu.VMEM((count, NZ, 16, HEAD), BF16),
            pltpu.VMEM((count, 16, HEAD), BF16),
            pltpu.VMEM((NZ, 16, HEAD), BF16),
        ]

    hbm = pl.BlockSpec(memory_space=pltpu.HBM)
    ring_buffers = [
        pltpu.VMEM((2, 8, 32, HEAD), BF16),
        pltpu.VMEM((2, 4, 32, HEAD), BF16),
        pltpu.VMEM((2, 8, 32, HEAD), BF16),
        pltpu.VMEM((4, 8, 32, HEAD), BF16),
    ]
    shapes = (
        jax.ShapeDtypeStruct((2, CAND, 512), BF16),
        jax.ShapeDtypeStruct((2, CAND, HEAD), BF16),
        jax.ShapeDtypeStruct((2, 16, HEAD), BF16),
        jax.ShapeDtypeStruct((2, 16, HEAD), BF16),
        jax.ShapeDtypeStruct((64, HEAD), F32),
    )
    results = pl.pallas_call(
        kernel,
        out_shape=shapes,
        in_specs=[hbm] * 7 + [smem, vmem, smem],
        out_specs=(hbm,) * 5,
        scratch_shapes=[
            *(pltpu.VMEM(one.shape, one.dtype) for one in shapes),
            pltpu.SemaphoreType.DMA((5,)),
            pltpu.VMEM((2, CAND, 512), BF16),
            pltpu.VMEM((2, CAND, HEAD), BF16),
            pltpu.VMEM((2, 16, HEAD), BF16),
            pltpu.VMEM((4, WIDTH), BF16),
            pltpu.VMEM((WIDTH, HEAD), BF16),
            pltpu.VMEM((2, CAND, 512), BF16),
            pltpu.SemaphoreType.DMA((7,)),
            pltpu.VMEM((16, 1024), F32),
            pltpu.VMEM((16, 1024), BF16),
            pltpu.VMEM((NZ, 32, 256), BF16),
            pltpu.VMEM((NY, 32, 256), BF16),
            pltpu.VMEM((NZ, 32, 256), BF16),
            pltpu.VMEM((NY, 32, 256), BF16),
            pltpu.VMEM((NZ, 2, 16, HEAD), BF16),
            pltpu.VMEM((NY, 2, 16, HEAD), BF16),
            pltpu.VMEM((NT, 32, WIDTH), BF16),
            pltpu.VMEM((NT, 16, 1024), BF16),
            pltpu.VMEM((2, 32, 16, HEAD), BF16),
            pltpu.VMEM((2, 32, 16, HEAD), BF16),
            pltpu.VMEM((HEAD, PREFIX), BF16),
            pltpu.VMEM((NYH, 8, 128), F32),
            pltpu.VMEM((NZ, 8, 128), F32),
            pltpu.VMEM((1024, HEAD), BF16),
            pltpu.VMEM((1024, HEAD), BF16),
            pltpu.VMEM((PREFIX + CAND, 1024), F32),
            pltpu.VMEM((2, CAND, HEAD), BF16),
            pltpu.VMEM((PREFIX, HEAD), F32),
            pltpu.VMEM((2, CAND, HEAD), F32),
            pltpu.VMEM((PREFIX, HEAD), F32),
            pltpu.VMEM((2, CAND, HEAD), F32),
            pltpu.VMEM((8, 2, 16, HEAD), F32),
            pltpu.VMEM((2, 32, 16, HEAD), BF16),
            pltpu.VMEM((2, 32, 16, HEAD), BF16),
            *small(NYH),
            *small(NYH),
            pltpu.VMEM((NYH, 16, HEAD), BF16),
            pltpu.VMEM((NZ, 16, HEAD), BF16),
            pltpu.VMEM((NYH, 16, HEAD), BF16),
            pltpu.VMEM((NZ, 16, HEAD), BF16),
            pltpu.VMEM((2, 64, 32, HEAD), BF16),
            *ring_buffers,
            *ring_buffers,
            pltpu.VMEM((NY, 32, HEAD), BF16),
            pltpu.VMEM((NZ, 32, HEAD), BF16),
            pltpu.VMEM((NY, 32, HEAD), BF16),
            pltpu.VMEM((NZ, 32, HEAD), BF16),
            pltpu.SemaphoreType.DMA((2, NT)),
            pltpu.SemaphoreType.DMA((2, NX)),
            pltpu.SemaphoreType.DMA((2, NX)),
            pltpu.SemaphoreType.DMA((2, 2, NZ)),
            pltpu.SemaphoreType.DMA((4, 2, NZ)),
            pltpu.SemaphoreType.DMA((4, 2, NZ)),
            pltpu.SemaphoreType.DMA((4, 2, NZ)),
            pltpu.SemaphoreType.DMA((4, 2, NZ)),
            pltpu.SemaphoreType.DMA((4, 2, NZ)),
            pltpu.SemaphoreType.DMA((2, 2, NZ)),
            pltpu.SemaphoreType.DMA((2, 2, NZ)),
            pltpu.SemaphoreType.DMA((2, 2, NZ)),
        ],
        compiler_params=pltpu.CompilerParams(
            collective_id=0, has_side_effects=True, vmem_limit_bytes=64 * 1024 * 1024
        ),
    )(
        cand_query[0],
        cand_key[0],
        shared_prefix_key.reshape(2, 16, HEAD),
        cand_hidden.reshape(32, WIDTH),
        prefix_hidden[0],
        value_matrix,
        out_cotangent[0],
        cand_scores,
        ranking,
        lengths,
    )
    gq, gck, gpk, gpv, gw = pl.pallas_call(
        hand_over,
        out_shape=shapes,
        in_specs=[pl.BlockSpec(memory_space=pl.ANY)] * 5,
        out_specs=(hbm,) * 5,
        scratch_shapes=[
            *(pltpu.VMEM(one.shape, one.dtype) for one in shapes),
            pltpu.SemaphoreType.DMA((2, 5)),
        ],
        compiler_params=pltpu.CompilerParams(vmem_limit_bytes=64 * 1024 * 1024),
    )(*results)
    return (
        gq[None],
        gck[None],
        gpk.reshape(1, 32, HEAD),
        gpv.reshape(1, 32, HEAD),
        gw,
    )


def solution(mesh):
    placed = (
        P("dp", "cand", None, "tensor"),
        P("dp", "cand", None, "tensor"),
        P("dp", "cand", "tensor"),
        P("dp", "cand", "tensor", None),
        P("dp", ("cand", "tensor"), None),
        P(None, "tensor"),
        P("dp", "cand", None, "tensor"),
        P("dp", "cand"),
        P("dp", None),
        P("dp", "cand"),
    )
    return jax.shard_map(
        shards,
        mesh=mesh,
        in_specs=placed,
        out_specs=(
            P("dp", "cand", None, "tensor"),
            P("dp", "cand", None, "tensor"),
            P("dp", "cand", "tensor"),
            P("dp", "cand", "tensor"),
            P(("dp", "cand"), "tensor"),
        ),
        check_vma=False,
    )
```

```python
import jax
import jax.numpy as jnp
from jax import lax
from jax.experimental import pallas as pl
from jax.experimental.pallas import tpu as pltpu
from jax.sharding import PartitionSpec as P

MESH = pl.DeviceIdType.MESH
BF16, F32 = jnp.bfloat16, jnp.float32
NZ, NYH, NY, NX, NT = 8, 4, 8, 4, 8
HEAD = 128
PREFIX = 1024
CAND = 128
CHUNK = 256
WIDTH = 4096
INV_ROOT = HEAD ** (-0.5)


def dot(a, b):
    return lax.dot_general(a, b, (((1,), (0,)), ((), ())), preferred_element_type=F32)


def dot_nt(a, b):
    return lax.dot_general(a, b, (((1,), (1,)), ((), ())), preferred_element_type=F32)


class Exchange:
    def __init__(self, n, me, device, src, dst, sems):
        self.n, self.me, self.device, self.src, self.dst, self.sems = n, me, device, src, dst, sems

    def copy(self, k, slot):
        peer = lax.rem(self.me + k, self.n)
        return pltpu.make_async_remote_copy(
            src_ref=self.src(peer),
            dst_ref=self.dst(slot),
            send_sem=self.sems.at[0, k],
            recv_sem=self.sems.at[1, k],
            device_id=self.device(peer),
            device_id_type=MESH,
        )

    def loop(self, step):
        def body(k, carry):
            step(k)
            return carry

        lax.fori_loop(1, self.n, body, 0)

    def start(self):
        self.loop(lambda k: self.copy(k, self.me).start())

    def wait_recv(self):
        self.loop(lambda k: self.copy(k, lax.rem(self.me + self.n - k, self.n)).wait_recv())

    def wait_send(self):
        self.loop(lambda k: self.copy(k, self.me).wait_send())


class Ring:
    def __init__(self, me, device, whole, half, third, fourth, joined, came, sems):
        self.me, self.device, self.whole, self.half = me, device, whole, half
        self.third, self.fourth, self.joined, self.came = third, fourth, joined, came

        def copy(i, src, dst, offset):
            return pltpu.make_async_remote_copy(
                src_ref=src,
                dst_ref=dst,
                send_sem=sems.at[0, i],
                recv_sem=sems.at[1, i],
                device_id=device(lax.rem(me + offset + 8, 8)),
                device_id_type=MESH,
            )

        self.first = (
            copy(0, self.block(3), third.at[0], 1),
            copy(1, self.block(-3), third.at[1], -1),
            copy(2, self.block(4, 0, 4), fourth.at[0], 2),
            copy(3, self.block(4, 4, 4), fourth.at[1], -2),
        )
        self.near = (
            copy(4, self.block(1), came.at[0], 1),
            copy(5, self.block(-1), came.at[1], -1),
        )
        self.second = (
            copy(6, joined.at[0], came.at[2], 2),
            copy(7, joined.at[1], came.at[3], -2),
        )

    def block(self, offset, start=0, count=8):
        slot = lax.rem(self.me + offset + 8, 8) * 8 + start
        return self.whole.at[self.half, pl.ds(slot, count)]

    def start(self):
        for one in self.first + self.near:
            one.start()

    def relay(self):
        for one in self.first:
            one.wait_recv()
        for side, offset in ((0, 2), (1, -2)):
            own = self.block(offset)[...].astype(F32) + self.third[side].astype(F32)
            part = slice(side * 4, side * 4 + 4)
            rest = slice(4 - side * 4, 8 - side * 4)
            self.joined[side, part] = (own[part] + self.fourth[side].astype(F32)).astype(BF16)
            self.joined[side, rest] = own[rest].astype(BF16)
            self.second[side].start()

    def total(self):
        result = self.block(0)[...].astype(F32)
        for i, one in enumerate(self.near + self.second):
            one.wait_recv()
            result = result + self.came[i].astype(F32)
        return result

    def wait_send(self):
        for one in self.first + self.near + self.second:
            one.wait_send()


def rank_gradient(scores_row, ranking_row):
    n = ranking_row.shape[1]
    rows = lax.broadcasted_iota(jnp.int32, (n, n), 0)
    cols = lax.broadcasted_iota(jnp.int32, (n, n), 1)
    scores_col = jnp.sum(jnp.where(rows == cols, scores_row, 0.0), axis=1, keepdims=True)
    picker = ranking_row == rows
    ordered = jnp.sum(jnp.where(picker, scores_col, 0.0), axis=0, keepdims=True)
    later = cols >= rows
    masked = jnp.where(later, ordered, -jnp.inf)
    top = jnp.max(masked, axis=1, keepdims=True)
    weights = jnp.exp(masked - top)
    suffix = weights / jnp.sum(weights, axis=1, keepdims=True)
    by_rank = jnp.sum(suffix, axis=0, keepdims=True) - 1.0
    return jnp.sum(jnp.where(picker, by_rank, 0.0), axis=1, keepdims=True)


def kernel(
    q_hbm, ck_hbm, pk_hbm, ch_hbm, ph_hbm, w_hbm, oc_hbm, sc_ref, rk_ref, ln_ref,
    gq_hbm, gck_hbm, gpk_hbm, gpv_hbm, gw_hbm,
    gq_ref, gck_ref, gpk_ref, gpv_ref, gw_ref, store_sem,
    q_ref, ck_ref, pk_ref, ph_ref, w_ref, oc_ref, load_sem,
    phs_ref, own_hp, sxa, sxb, xa, xb, ga, gb,
    hc_ref, hp_ref, kall_ref, vall_ref, kt_ref, s1_ref, s2_ref,
    qs_ref, cs_ref, p_ref, vc_ref, dvp_ref, dvc_ref, dkp_ref, dkc_ref, dvr_ref,
    send_v, send_k, rva1, rvb1, rva2, rvb2, rka1, rkb1, rka2, rkb2, tva2, tvb2, tka2, tkb2,
    send_w, third_a, fourth_a, joined_a, came_a, third_b, fourth_b, joined_b, came_b,
    rwa2, rwb2, twa2, twb2,
    sem_hp, sem_hx, sem_hs, sem_s, sem_k, sem_v, sem_dv, sem_dk, sem_dw, sem_r, sem_x, sem_g,
):
    dp = lax.axis_index("dp")
    cand = lax.axis_index("cand")
    tens = lax.axis_index("tensor")
    z, yh = cand // NYH, lax.rem(cand, NYH)
    y = yh * 2 + dp
    x, core = tens // 2, lax.rem(tens, 2)
    other = 1 - core

    def at_t(t):
        return (dp, cand, t)

    def at_x(xx):
        return (dp, cand, xx * 2 + core)

    def at_z(zz):
        return (dp, zz * NYH + yh, tens)

    def at_yh(yy):
        return (dp, z * NYH + yy, tens)

    def at_y(yy):
        return (lax.rem(yy, 2), z * NYH + yy // 2, tens)

    barrier = pltpu.get_barrier_semaphore()
    for n, me, device in ((NT, tens, at_t), (NZ, z, at_z), (NY, y, at_y)):
        def greet(k, carry, n=n, me=me, device=device):
            pl.semaphore_signal(
                barrier, inc=1, device_id=device(lax.rem(me + k, n)), device_id_type=MESH
            )
            return carry

        lax.fori_loop(1, n, greet, 0)

    loads = [
        pltpu.make_async_copy(src, dst, load_sem.at[i])
        for i, (src, dst) in enumerate((
            (pk_hbm, pk_ref), (ph_hbm, ph_ref), (ch_hbm, hc_ref.at[tens]), (q_hbm, q_ref),
            (ck_hbm, ck_ref), (w_hbm, w_ref), (oc_hbm, oc_ref),
        ))
    ]
    for load in loads:
        load.start()
    stores = [
        pltpu.make_async_copy(src, dst, store_sem.at[i])
        for i, (src, dst) in enumerate((
            (gq_ref, gq_hbm), (gck_ref, gck_hbm), (gpk_ref, gpk_hbm), (gpv_ref, gpv_hbm),
            (gw_ref, gw_hbm),
        ))
    ]

    loads[0].wait()
    kall_ref[0, z * NYH + yh] = pk_ref[0]
    kall_ref[1, yh * NZ + z] = pk_ref[1]
    loads[1].wait()
    own_rows = ph_ref[...].astype(F32)
    for b in range(4):
        phs_ref[b * 4:(b + 1) * 4, :] = own_rows[:, b * 1024:(b + 1) * 1024]
    own_hp[...] = phs_ref[...].astype(BF16)
    hp_ref[tens] = own_hp[...]
    loads[2].wait()
    loads[3].wait()
    lane = lax.broadcasted_iota(jnp.int32, (8, 128), 1)
    own_scores = jnp.where(
        lane == 2 * cand, sc_ref[0, 0], jnp.where(lane == 2 * cand + 1, sc_ref[0, 1], 0.0)
    )
    s1_ref[yh] = own_scores
    for c in range(2):
        for r in range(4):
            base = c * 512 + r * 128
            qs_ref[base:base + 128, :] = q_ref[c, :, r * 128:(r + 1) * 128]
    dvp_ref[...] = jnp.zeros_like(dvp_ref)
    dvc_ref[...] = jnp.zeros_like(dvc_ref)
    dkp_ref[...] = jnp.zeros_like(dkp_ref)
    dkc_ref[...] = jnp.zeros_like(dkc_ref)
    for load in loads[4:]:
        load.wait()

    pl.semaphore_wait(barrier, (NT - 1) + (NZ - 1) + (NY - 1))

    def gather(own, whole, sems):
        a1 = Exchange(NYH, yh, at_yh, lambda p: own.at[0],
                      lambda s: whole.at[0, z * NYH + s], sems.at[0])
        b1 = Exchange(NZ, z, at_z, lambda p: own.at[1],
                      lambda s: whole.at[1, yh * NZ + s], sems.at[1])
        a2 = Exchange(NZ, z, at_z, lambda p: whole.at[0, pl.ds(z * NYH, NYH)],
                      lambda s: whole.at[0, pl.ds(s * NYH, NYH)], sems.at[2])
        b2 = Exchange(NYH, yh, at_yh, lambda p: whole.at[1, pl.ds(yh * NZ, NZ)],
                      lambda s: whole.at[1, pl.ds(s * NZ, NZ)], sems.at[3])
        return a1, b1, a2, b2

    hp_x = Exchange(NT, tens, at_t, lambda p: own_hp, lambda s: hp_ref.at[s], sem_hp)
    left, right = lax.rem(x + NX - 1, NX), lax.rem(x + 1, NX)
    across = lax.rem(x + 2, NX)

    def along(sem, block, rows, to):
        return pltpu.make_async_remote_copy(
            src_ref=hc_ref.at[block * 2 + core, rows],
            dst_ref=hc_ref.at[block * 2 + core, rows],
            send_sem=sem_hx.at[0, sem],
            recv_sem=sem_hx.at[1, sem],
            device_id=at_x(to),
            device_id_type=MESH,
        )

    both, upper, lower = pl.ds(0, 32), pl.ds(0, 16), pl.ds(16, 16)
    hc_sent = (
        along(0, x, both, right), along(1, x, both, left),
        along(2, left, upper, right), along(3, right, lower, left),
    )
    hc_came = (
        along(0, left, both, right), along(1, right, both, left),
        along(2, across, upper, right), along(3, across, lower, left),
    )
    s_1 = Exchange(NYH, yh, at_yh, lambda p: s1_ref.at[yh], lambda s: s1_ref.at[s], sem_s.at[0])
    s_2 = Exchange(NZ, z, at_z, lambda p: s2_ref.at[z], lambda s: s2_ref.at[s], sem_s.at[1])
    k_a1, k_b1, k_a2, k_b2 = gather(pk_ref, kall_ref, sem_k)

    def sibling(xx, mine):
        slot = xx * 2 + (core if mine else other)
        return pltpu.make_async_remote_copy(
            src_ref=hc_ref.at[xx * 2 + core],
            dst_ref=hc_ref.at[slot],
            send_sem=sem_hs.at[0, xx],
            recv_sem=sem_hs.at[1, xx],
            device_id=(dp, cand, x * 2 + other),
            device_id_type=MESH,
        )

    k_a1.start()
    k_b1.start()
    s_1.start()
    hp_x.start()
    hc_sent[0].start()
    hc_sent[1].start()
    sibling(x, True).start()

    k_a1.wait_recv()
    k_a2.start()
    k_b1.wait_recv()
    k_b2.start()
    s_1.wait_recv()
    s2_ref[z] = s1_ref[0] + s1_ref[1] + s1_ref[2] + s1_ref[3]
    s_2.start()

    hp_x.wait_recv()
    to = lax.broadcasted_iota(jnp.int32, (128, 128), 0)
    came = lax.broadcasted_iota(jnp.int32, (128, 128), 1)
    order = came == lax.rem(to // 4, 8) * 16 + (to // 32) * 4 + lax.rem(to, 4)
    hp_rows = dot(
        jnp.where(order, 1.0, 0.0).astype(BF16), hp_ref[...].reshape(128, 1024)
    ).astype(BF16)
    pv = jnp.zeros((32, HEAD), F32)
    for b in range(4):
        pv = pv + dot(hp_rows[b * 32:(b + 1) * 32], w_ref[b * 1024:(b + 1) * 1024, :])
    pv = pv.astype(BF16).reshape(2, 16, HEAD)
    vall_ref[0, z * NYH + yh] = pv[0]
    vall_ref[1, yh * NZ + z] = pv[1]

    class Own:
        def __init__(self, first, second):
            self.at = (first, second)

    v_a1, v_b1, v_a2, v_b2 = gather(
        Own(vall_ref.at[0, z * NYH + yh], vall_ref.at[1, yh * NZ + z]), vall_ref, sem_v
    )
    v_a1.start()
    v_b1.start()

    spot = lax.broadcasted_iota(jnp.int32, (1, 1024), 1)
    place = lax.rem(spot, 512)
    outer, inner, last = place // 128, lax.rem(place // 32, 4), lax.rem(spot, 32)
    wanted = jnp.where(
        spot < 512, outer * 256 + inner * 64 + last, inner * 256 + outer * 64 + 32 + last
    )
    sorted_hp = jnp.zeros((128, 1024), F32)
    for b in range(4):
        row = lax.broadcasted_iota(jnp.int32, (256, 1024), 0) + b * 256
        pick = jnp.where(row == wanted, 1.0, 0.0).astype(BF16)
        sorted_hp = sorted_hp + dot(hp_rows[:, b * 256:(b + 1) * 256], pick)
    sorted_hp = sorted_hp.astype(BF16)
    for d in range(2):
        for zh in range(2):
            rows = sorted_hp[(d * 2 + zh) * 32:(d * 2 + zh + 1) * 32]
            for j in range(4):
                sxa[zh * 4 + j, :, d * 128:(d + 1) * 128] = rows[:, j * 128:(j + 1) * 128]
                sxb[j * 2 + d, :, zh * 128:(zh + 1) * 128] = (
                    rows[:, 512 + j * 128:512 + (j + 1) * 128]
                )
    xa[z] = sxa[z]
    xb[y] = sxb[y]
    x_a = Exchange(NZ, z, at_z, lambda p: sxa.at[p], lambda s: xa.at[s], sem_x.at[0])
    x_b = Exchange(NY, y, at_y, lambda p: sxb.at[p], lambda s: xb.at[s], sem_x.at[1])
    x_a.start()
    x_b.start()

    for i, block in ((0, left), (1, right)):
        hc_came[i].wait_recv()
        hc_sent[i + 2].start()
        sibling(block, True).start()

    s_2.wait_recv()
    total = s2_ref[0]
    for i in range(1, NZ):
        total = total + s2_ref[i]
    list_grad = rank_gradient(total[0:1, 0:64], rk_ref[...])
    item = lax.broadcasted_iota(jnp.int32, (64, 1), 0)
    for c in range(2):
        own_grad = jnp.sum(
            jnp.where(item == 2 * cand + c, list_grad, 0.0), axis=0, keepdims=True
        )
        live = lax.broadcasted_iota(jnp.int32, (CAND, 128), 0) < ln_ref[0, c]
        for r in range(4):
            base = c * 512 + r * 128
            part = oc_ref[c, :, r * 128:(r + 1) * 128].astype(F32) * own_grad
            cs_ref[base:base + 128, :] = jnp.where(live, part, 0.0).astype(BF16)

    k_a2.wait_recv()
    k_b2.wait_recv()
    kt_ref[...] = kall_ref[...].reshape(PREFIX, HEAD).astype(F32).T.astype(BF16)

    def soft(n, carry):
        c = n // 2
        cols = pl.ds(pl.multiple_of(n * CHUNK, CHUNK), CHUNK)
        queries = qs_ref[cols, :]
        cot = cs_ref[cols, :]
        log_p = dot_nt(kall_ref[...].reshape(PREFIX, HEAD), queries) * INV_ROOT
        log_c = dot_nt(ck_ref[c], queries) * INV_ROOT
        slot = lax.broadcasted_iota(jnp.int32, (CAND, CHUNK), 0)
        position = lax.rem(lax.broadcasted_iota(jnp.int32, (CAND, CHUNK), 1), CAND)
        allowed = (slot <= position) & (slot < ln_ref[0, c])
        log_c = jnp.where(allowed, log_c, -jnp.inf)
        top = jnp.maximum(
            jnp.max(log_p, axis=0, keepdims=True), jnp.max(log_c, axis=0, keepdims=True)
        )
        exp_p = jnp.exp(log_p - top)
        exp_c = jnp.exp(log_c - top)
        inverse = 1.0 / (
            jnp.sum(exp_p, axis=0, keepdims=True) + jnp.sum(exp_c, axis=0, keepdims=True)
        )
        prob_p = exp_p * inverse
        prob_c = exp_c * inverse
        p_ref[0:PREFIX, cols] = prob_p
        p_ref[PREFIX:PREFIX + CAND, cols] = prob_c
        dvp_ref[...] += dot(prob_p.astype(BF16), cot)
        dvc_ref[c] += dot(prob_c.astype(BF16), cot)
        return carry

    lax.fori_loop(0, 1, soft, 0, unroll=True)
    lax.fori_loop(1, 2, soft, 0, unroll=True)
    v_a1.wait_recv()
    v_a2.start()
    v_b1.wait_recv()
    v_b2.start()
    hc_came[2].wait_recv()
    hc_came[3].wait_recv()
    sibling(across, True).start()
    lax.fori_loop(2, 4, soft, 0, unroll=True)

    def scatter(whole, ra1, rb1, ra2, rb2, ta2, tb2, sems, ny, my_y, at_group):
        a1 = Exchange(NZ, z, at_z, lambda p: whole.at[0, pl.ds(p * ny, ny)],
                      lambda s: ra1.at[s], sems.at[0])
        b1 = Exchange(ny, my_y, at_group, lambda p: whole.at[1, pl.ds(p * NZ, NZ)],
                      lambda s: rb1.at[s], sems.at[1])
        a2 = Exchange(ny, my_y, at_group, lambda p: ta2.at[p], lambda s: ra2.at[s], sems.at[2])
        b2 = Exchange(NZ, z, at_z, lambda p: tb2.at[p], lambda s: rb2.at[s], sems.at[3])

        def middle():
            a1.wait_recv()
            ra1[z] = whole[0, pl.ds(z * ny, ny)]
            total = ra1[0].astype(F32)
            for i in range(1, NZ):
                total = total + ra1[i].astype(F32)
            ta2[...] = total.astype(BF16)
            a2.start()
            b1.wait_recv()
            rb1[my_y] = whole[1, pl.ds(my_y * NZ, NZ)]
            total = rb1[0].astype(F32)
            for i in range(1, ny):
                total = total + rb1[i].astype(F32)
            tb2[...] = total.astype(BF16)
            b2.start()

        def end():
            a2.wait_recv()
            ra2[my_y] = ta2[my_y]
            first = ra2[0].astype(F32)
            for i in range(1, ny):
                first = first + ra2[i].astype(F32)
            b2.wait_recv()
            rb2[z] = tb2[z]
            second = rb2[0].astype(F32)
            for i in range(1, NZ):
                second = second + rb2[i].astype(F32)
            return first, second

        return (a1, b1, a2, b2), middle, end

    dv_all, dv_middle, dv_end = scatter(
        send_v, rva1, rvb1, rva2, rvb2, tva2, tvb2, sem_dv, NYH, yh, at_yh
    )
    send_v[...] = dvp_ref[...].astype(BF16).reshape(2, 32, 16, HEAD)
    dv_all[0].start()
    dv_all[1].start()

    def from_sibling(k, carry):
        sibling(k, False).wait_recv()
        return carry

    lax.fori_loop(0, NX, from_sibling, 0)
    for c in range(2):
        dvr_ref[:, c] = dvc_ref[c].reshape(8, 16, HEAD)
    dvr_t = dvr_ref[...].reshape(256, HEAD).T.astype(BF16)

    def weight(b, carry):
        cols = pl.ds(pl.multiple_of(b * 512, 512), 512)
        part = dot(dvr_t, hc_ref[:, :, cols].reshape(256, 512))
        rows = part.T.astype(BF16).reshape(2, NYH, 2, 32, HEAD)
        d, zz = b // 4, lax.rem(b, 4) * 2
        for i in range(2):
            for j in range(NYH):
                send_w[0, (zz + i) * NY + j * 2 + d] = rows[i, j, 0]
                send_w[1, (j * 2 + d) * NZ + zz + i] = rows[i, j, 1]
        return carry

    lax.fori_loop(0, 8, weight, 0)
    ring_a = Ring(z, at_z, send_w, 0, third_a, fourth_a, joined_a, came_a, sem_r.at[0])
    ring_b = Ring(y, at_y, send_w, 1, third_b, fourth_b, joined_b, came_b, sem_r.at[1])
    dw_a = Exchange(NY, y, at_y, lambda p: twa2.at[p], lambda s: rwa2.at[s], sem_dw.at[0])
    dw_b = Exchange(NZ, z, at_z, lambda p: twb2.at[p], lambda s: rwb2.at[s], sem_dw.at[1])
    ring_a.start()
    ring_b.start()
    dv_middle()

    cv = dot(hc_ref[...].reshape(256, WIDTH), w_ref[...]).astype(BF16).reshape(8, 2, 16, HEAD)
    for c in range(2):
        vc_ref[c] = cv[:, c].reshape(CAND, HEAD)
    v_a2.wait_recv()
    v_b2.wait_recv()

    def score(n, carry):
        c = n // 2
        cols = pl.ds(pl.multiple_of(n * CHUNK, CHUNK), CHUNK)
        queries = qs_ref[cols, :]
        cot = cs_ref[cols, :]
        dprob_p = dot_nt(vall_ref[...].reshape(PREFIX, HEAD), cot)
        dprob_c = dot_nt(vc_ref[c], cot)
        prob_p = p_ref[0:PREFIX, cols]
        prob_c = p_ref[PREFIX:PREFIX + CAND, cols]
        row_total = jnp.sum(prob_p * dprob_p, axis=0, keepdims=True) + jnp.sum(
            prob_c * dprob_c, axis=0, keepdims=True
        )
        ds_p = (prob_p * (dprob_p - row_total)).astype(BF16)
        ds_c = (prob_c * (dprob_c - row_total)).astype(BF16)
        dkp_ref[...] += dot(ds_p, queries)
        dkc_ref[c] += dot(ds_c, queries)
        kc_t = ck_ref[c].astype(F32).T.astype(BF16)
        gq_t = (dot(kt_ref[...], ds_p) + dot(kc_t, ds_c)) * INV_ROOT
        p_ref[0:128, cols] = gq_t
        return carry

    lax.fori_loop(0, 1, score, 0, unroll=True)
    ring_a.relay()
    ring_b.relay()
    lax.fori_loop(1, 2, score, 0, unroll=True)

    first, second = dv_end()
    gpv_ref[0] = first.astype(BF16)
    gpv_ref[1] = second.astype(BF16)
    stores[3].start()
    ga[z] = gpv_ref[...]
    gb[y] = gpv_ref[...]
    g_a = Exchange(NZ, z, at_z, lambda p: ga.at[z], lambda s: ga.at[s], sem_g.at[0])
    g_b = Exchange(NY, y, at_y, lambda p: gb.at[y], lambda s: gb.at[s], sem_g.at[1])
    g_a.start()
    g_b.start()
    lax.fori_loop(2, 4, score, 0, unroll=True)

    dk_all, dk_middle, dk_end = scatter(
        send_k, rka1, rkb1, rka2, rkb2, tka2, tkb2, sem_dk, NYH, yh, at_yh
    )
    send_k[...] = (dkp_ref[...] * INV_ROOT).astype(BF16).reshape(2, 32, 16, HEAD)
    dk_all[0].start()
    dk_all[1].start()

    for c in range(2):
        gck_ref[c] = (dkc_ref[c] * INV_ROOT).astype(BF16)
        for r in range(4):
            base = c * 512 + r * 128
            gq_ref[c, :, r * 128:(r + 1) * 128] = (
                p_ref[0:128, base:base + 128].T.astype(BF16)
            )
    stores[0].start()
    stores[1].start()

    x_a.wait_recv()
    x_b.wait_recv()

    def prefix_part(half):
        (g_a, g_b)[half].wait_recv()
        rows = (ga, gb)[half][...].reshape(256, HEAD).astype(F32).T.astype(BF16)
        part = dot(rows, (xa, xb)[half][...].reshape(256, 256))
        part = part.T
        if half == 0:
            part = part.reshape(2, NYH, 32, HEAD).swapaxes(0, 1)
        return part.reshape(8, 32, HEAD)

    twa2[...] = (ring_a.total() + prefix_part(0)).astype(BF16)
    dw_a.start()
    twb2[...] = (ring_b.total() + prefix_part(1)).astype(BF16)
    dw_b.start()
    dk_middle()
    first, second = dk_end()
    gpk_ref[0] = first.astype(BF16)
    gpk_ref[1] = second.astype(BF16)
    stores[2].start()
    for i, (one, mine, sent, came) in enumerate(((dw_a, y, twa2, rwa2), (dw_b, z, twb2, rwb2))):
        one.wait_recv()
        came[mine] = sent[mine]
        last = came[0].astype(F32)
        for j in range(1, 8):
            last = last + came[j].astype(F32)
        gw_ref[i * 32:(i + 1) * 32, :] = last
    stores[4].start()

    for group in (
        (*hc_sent, hp_x, s_1, s_2, k_a1, k_b1, k_a2, k_b2, v_a1, v_b1, v_a2, v_b2,
         x_a, x_b, g_a, g_b),
        (ring_a, ring_b, dw_a, dw_b), dv_all, dk_all,
    ):
        for one in group:
            one.wait_send()

    def sent(k, carry):
        sibling(k, True).wait_send()
        return carry

    lax.fori_loop(0, NX, sent, 0)
    for store in stores:
        store.wait()


def hand_over(*refs):
    sources, results, held, sems = refs[:5], refs[5:10], refs[10:15], refs[15]
    loads = [pltpu.make_async_copy(a, b, sems.at[0, i]) for i, (a, b) in enumerate(zip(sources, held))]
    stores = [pltpu.make_async_copy(a, b, sems.at[1, i]) for i, (a, b) in enumerate(zip(held, results))]
    for load in loads:
        load.start()
    for load, store in zip(loads, stores):
        load.wait()
        store.start()
    for store in stores:
        store.wait()


def shards(
    cand_query, cand_key, shared_prefix_key, cand_hidden, prefix_hidden, value_matrix,
    out_cotangent, cand_scores, ranking, lengths,
):
    vmem = pl.BlockSpec(memory_space=pltpu.VMEM)
    smem = pl.BlockSpec(memory_space=pltpu.SMEM)

    def small(count):
        return [
            pltpu.VMEM((NZ, count, 16, HEAD), BF16),
            pltpu.VMEM((count, NZ, 16, HEAD), BF16),
            pltpu.VMEM((count, 16, HEAD), BF16),
            pltpu.VMEM((NZ, 16, HEAD), BF16),
        ]

    hbm = pl.BlockSpec(memory_space=pltpu.HBM)
    ring_buffers = [
        pltpu.VMEM((2, 8, 32, HEAD), BF16),
        pltpu.VMEM((2, 4, 32, HEAD), BF16),
        pltpu.VMEM((2, 8, 32, HEAD), BF16),
        pltpu.VMEM((4, 8, 32, HEAD), BF16),
    ]
    shapes = (
        jax.ShapeDtypeStruct((2, CAND, 512), BF16),
        jax.ShapeDtypeStruct((2, CAND, HEAD), BF16),
        jax.ShapeDtypeStruct((2, 16, HEAD), BF16),
        jax.ShapeDtypeStruct((2, 16, HEAD), BF16),
        jax.ShapeDtypeStruct((64, HEAD), F32),
    )
    results = pl.pallas_call(
        kernel,
        out_shape=shapes,
        in_specs=[hbm] * 7 + [smem, vmem, smem],
        out_specs=(hbm,) * 5,
        scratch_shapes=[
            *(pltpu.VMEM(one.shape, one.dtype) for one in shapes),
            pltpu.SemaphoreType.DMA((5,)),
            pltpu.VMEM((2, CAND, 512), BF16),
            pltpu.VMEM((2, CAND, HEAD), BF16),
            pltpu.VMEM((2, 16, HEAD), BF16),
            pltpu.VMEM((4, WIDTH), BF16),
            pltpu.VMEM((WIDTH, HEAD), BF16),
            pltpu.VMEM((2, CAND, 512), BF16),
            pltpu.SemaphoreType.DMA((7,)),
            pltpu.VMEM((16, 1024), F32),
            pltpu.VMEM((16, 1024), BF16),
            pltpu.VMEM((NZ, 32, 256), BF16),
            pltpu.VMEM((NY, 32, 256), BF16),
            pltpu.VMEM((NZ, 32, 256), BF16),
            pltpu.VMEM((NY, 32, 256), BF16),
            pltpu.VMEM((NZ, 2, 16, HEAD), BF16),
            pltpu.VMEM((NY, 2, 16, HEAD), BF16),
            pltpu.VMEM((NT, 32, WIDTH), BF16),
            pltpu.VMEM((NT, 16, 1024), BF16),
            pltpu.VMEM((2, 32, 16, HEAD), BF16),
            pltpu.VMEM((2, 32, 16, HEAD), BF16),
            pltpu.VMEM((HEAD, PREFIX), BF16),
            pltpu.VMEM((NYH, 8, 128), F32),
            pltpu.VMEM((NZ, 8, 128), F32),
            pltpu.VMEM((1024, HEAD), BF16),
            pltpu.VMEM((1024, HEAD), BF16),
            pltpu.VMEM((PREFIX + CAND, 1024), F32),
            pltpu.VMEM((2, CAND, HEAD), BF16),
            pltpu.VMEM((PREFIX, HEAD), F32),
            pltpu.VMEM((2, CAND, HEAD), F32),
            pltpu.VMEM((PREFIX, HEAD), F32),
            pltpu.VMEM((2, CAND, HEAD), F32),
            pltpu.VMEM((8, 2, 16, HEAD), F32),
            pltpu.VMEM((2, 32, 16, HEAD), BF16),
            pltpu.VMEM((2, 32, 16, HEAD), BF16),
            *small(NYH),
            *small(NYH),
            pltpu.VMEM((NYH, 16, HEAD), BF16),
            pltpu.VMEM((NZ, 16, HEAD), BF16),
            pltpu.VMEM((NYH, 16, HEAD), BF16),
            pltpu.VMEM((NZ, 16, HEAD), BF16),
            pltpu.VMEM((2, 64, 32, HEAD), BF16),
            *ring_buffers,
            *ring_buffers,
            pltpu.VMEM((NY, 32, HEAD), BF16),
            pltpu.VMEM((NZ, 32, HEAD), BF16),
            pltpu.VMEM((NY, 32, HEAD), BF16),
            pltpu.VMEM((NZ, 32, HEAD), BF16),
            pltpu.SemaphoreType.DMA((2, NT)),
            pltpu.SemaphoreType.DMA((2, NX)),
            pltpu.SemaphoreType.DMA((2, NX)),
            pltpu.SemaphoreType.DMA((2, 2, NZ)),
            pltpu.SemaphoreType.DMA((4, 2, NZ)),
            pltpu.SemaphoreType.DMA((4, 2, NZ)),
            pltpu.SemaphoreType.DMA((4, 2, NZ)),
            pltpu.SemaphoreType.DMA((4, 2, NZ)),
            pltpu.SemaphoreType.DMA((4, 2, NZ)),
            pltpu.SemaphoreType.DMA((2, 2, NZ)),
            pltpu.SemaphoreType.DMA((2, 2, NZ)),
            pltpu.SemaphoreType.DMA((2, 2, NZ)),
        ],
        compiler_params=pltpu.CompilerParams(
            collective_id=0, has_side_effects=True, vmem_limit_bytes=64 * 1024 * 1024
        ),
    )(
        cand_query[0],
        cand_key[0],
        shared_prefix_key.reshape(2, 16, HEAD),
        cand_hidden.reshape(32, WIDTH),
        prefix_hidden[0],
        value_matrix,
        out_cotangent[0],
        cand_scores,
        ranking,
        lengths,
    )
    gq, gck, gpk, gpv, gw = pl.pallas_call(
        hand_over,
        out_shape=shapes,
        in_specs=[pl.BlockSpec(memory_space=pl.ANY)] * 5,
        out_specs=(hbm,) * 5,
        scratch_shapes=[
            *(pltpu.VMEM(one.shape, one.dtype) for one in shapes),
            pltpu.SemaphoreType.DMA((2, 5)),
        ],
        compiler_params=pltpu.CompilerParams(vmem_limit_bytes=64 * 1024 * 1024),
    )(*results)
    return (
        gq[None],
        gck[None],
        gpk.reshape(1, 32, HEAD),
        gpv.reshape(1, 32, HEAD),
        gw,
    )


def solution(mesh):
    placed = (
        P("dp", "cand", None, "tensor"),
        P("dp", "cand", None, "tensor"),
        P("dp", "cand", "tensor"),
        P("dp", "cand", "tensor", None),
        P("dp", ("cand", "tensor"), None),
        P(None, "tensor"),
        P("dp", "cand", None, "tensor"),
        P("dp", "cand"),
        P("dp", None),
        P("dp", "cand"),
    )
    return jax.shard_map(
        shards,
        mesh=mesh,
        in_specs=placed,
        out_specs=(
            P("dp", "cand", None, "tensor"),
            P("dp", "cand", None, "tensor"),
            P("dp", "cand", "tensor"),
            P("dp", "cand", "tensor"),
            P(("dp", "cand"), "tensor"),
        ),
        check_vma=False,
    )
```

```python
import jax
import jax.numpy as jnp
from jax import lax
from jax.experimental import pallas as pl
from jax.experimental.pallas import tpu as pltpu
from jax.sharding import PartitionSpec as P

MESH = pl.DeviceIdType.MESH
BF16, F32 = jnp.bfloat16, jnp.float32
NZ, NYH, NY, NX, NT = 8, 4, 8, 4, 8
HEAD = 128
PREFIX = 1024
CAND = 128
CHUNK = 256
WIDTH = 4096
INV_ROOT = HEAD ** (-0.5)
EXP_SCALE = INV_ROOT * 1.4426950408889634


def dot(a, b):
    return lax.dot_general(a, b, (((1,), (0,)), ((), ())), preferred_element_type=F32)


def dot_nt(a, b):
    return lax.dot_general(a, b, (((1,), (1,)), ((), ())), preferred_element_type=F32)


class Exchange:
    def __init__(self, n, me, device, src, dst, sems):
        self.n, self.me, self.device, self.src, self.dst, self.sems = n, me, device, src, dst, sems

    def copy(self, k, slot):
        peer = lax.rem(self.me + k, self.n)
        return pltpu.make_async_remote_copy(
            src_ref=self.src(peer),
            dst_ref=self.dst(slot),
            send_sem=self.sems.at[0, k],
            recv_sem=self.sems.at[1, k],
            device_id=self.device(peer),
            device_id_type=MESH,
        )

    def loop(self, step):
        def body(k, carry):
            step(k)
            return carry

        lax.fori_loop(1, self.n, body, 0)

    def start(self):
        self.loop(lambda k: self.copy(k, self.me).start())

    def wait_recv(self):
        self.loop(lambda k: self.copy(k, lax.rem(self.me + self.n - k, self.n)).wait_recv())

    def wait_send(self):
        self.loop(lambda k: self.copy(k, self.me).wait_send())


class Ring:
    def __init__(self, me, device, whole, half, third, fourth, joined, came, sems):
        self.me, self.device, self.whole, self.half = me, device, whole, half
        self.third, self.fourth, self.joined, self.came = third, fourth, joined, came

        def copy(i, src, dst, offset):
            return pltpu.make_async_remote_copy(
                src_ref=src,
                dst_ref=dst,
                send_sem=sems.at[0, i],
                recv_sem=sems.at[1, i],
                device_id=device(lax.rem(me + offset + 8, 8)),
                device_id_type=MESH,
            )

        self.first = (
            copy(0, self.block(3), third.at[0], 1),
            copy(1, self.block(-3), third.at[1], -1),
            copy(2, self.block(4, 0, 4), fourth.at[0], 2),
            copy(3, self.block(4, 4, 4), fourth.at[1], -2),
        )
        self.near = (
            copy(4, self.block(1), came.at[0], 1),
            copy(5, self.block(-1), came.at[1], -1),
        )
        self.second = (
            copy(6, joined.at[0], came.at[2], 2),
            copy(7, joined.at[1], came.at[3], -2),
        )

    def block(self, offset, start=0, count=8):
        slot = lax.rem(self.me + offset + 8, 8) * 8 + start
        return self.whole.at[self.half, pl.ds(slot, count)]

    def start(self):
        for one in self.first + self.near:
            one.start()

    def relay(self):
        for one in self.first:
            one.wait_recv()
        for side, offset in ((0, 2), (1, -2)):
            own = self.block(offset)[...].astype(F32) + self.third[side].astype(F32)
            part = slice(side * 4, side * 4 + 4)
            rest = slice(4 - side * 4, 8 - side * 4)
            self.joined[side, part] = (own[part] + self.fourth[side].astype(F32)).astype(BF16)
            self.joined[side, rest] = own[rest].astype(BF16)
            self.second[side].start()

    def total(self):
        result = self.block(0)[...].astype(F32)
        for i, one in enumerate(self.near + self.second):
            one.wait_recv()
            result = result + self.came[i].astype(F32)
        return result

    def wait_send(self):
        for one in self.first + self.near + self.second:
            one.wait_send()


def rank_gradient(scores_row, ranking_row):
    n = ranking_row.shape[1]
    rows = lax.broadcasted_iota(jnp.int32, (n, n), 0)
    cols = lax.broadcasted_iota(jnp.int32, (n, n), 1)
    scores_col = jnp.sum(jnp.where(rows == cols, scores_row, 0.0), axis=1, keepdims=True)
    picker = ranking_row == rows
    ordered = jnp.sum(jnp.where(picker, scores_col, 0.0), axis=0, keepdims=True)
    later = cols >= rows
    masked = jnp.where(later, ordered, -jnp.inf)
    top = jnp.max(masked, axis=1, keepdims=True)
    weights = jnp.exp(masked - top)
    suffix = weights / jnp.sum(weights, axis=1, keepdims=True)
    by_rank = jnp.sum(suffix, axis=0, keepdims=True) - 1.0
    return jnp.sum(jnp.where(picker, by_rank, 0.0), axis=1, keepdims=True)


def kernel(
    q_hbm, ck_hbm, pk_hbm, ch_hbm, ph_hbm, w_hbm, oc_hbm, sc_ref, rk_ref, ln_ref,
    gq_hbm, gck_hbm, gpk_hbm, gpv_hbm, gw_hbm,
    gq_ref, gck_ref, gpk_ref, gpv_ref, gw_ref, store_sem,
    q_ref, ck_ref, pk_ref, ph_ref, w_ref, oc_ref, load_sem,
    phs_ref, own_hp, sxa, sxb, xa, xb, ga, gb,
    hc_ref, hp_ref, kall_ref, vall_ref, kt_ref, s1_ref, s2_ref,
    qs_ref, cs_ref, p_ref, vc_ref, dvp_ref, dvc_ref, dkp_ref, dkc_ref, dvr_ref,
    send_v, send_k, rva1, rvb1, rva2, rvb2, rka1, rkb1, rka2, rkb2, tva2, tvb2, tka2, tkb2,
    send_w, third_a, fourth_a, joined_a, came_a, third_b, fourth_b, joined_b, came_b,
    rwa2, rwb2, twa2, twb2,
    sem_hp, sem_hx, sem_hs, sem_s, sem_k, sem_v, sem_dv, sem_dk, sem_dw, sem_r, sem_x, sem_g,
):
    dp = lax.axis_index("dp")
    cand = lax.axis_index("cand")
    tens = lax.axis_index("tensor")
    z, yh = cand // NYH, lax.rem(cand, NYH)
    y = yh * 2 + dp
    x, core = tens // 2, lax.rem(tens, 2)
    other = 1 - core

    def at_t(t):
        return (dp, cand, t)

    def at_x(xx):
        return (dp, cand, xx * 2 + core)

    def at_z(zz):
        return (dp, zz * NYH + yh, tens)

    def at_yh(yy):
        return (dp, z * NYH + yy, tens)

    def at_y(yy):
        return (lax.rem(yy, 2), z * NYH + yy // 2, tens)

    barrier = pltpu.get_barrier_semaphore()
    for n, me, device in ((NT, tens, at_t), (NZ, z, at_z), (NY, y, at_y)):
        def greet(k, carry, n=n, me=me, device=device):
            pl.semaphore_signal(
                barrier, inc=1, device_id=device(lax.rem(me + k, n)), device_id_type=MESH
            )
            return carry

        lax.fori_loop(1, n, greet, 0)

    loads = [
        pltpu.make_async_copy(src, dst, load_sem.at[i])
        for i, (src, dst) in enumerate((
            (pk_hbm, pk_ref), (ph_hbm, ph_ref), (ch_hbm, hc_ref.at[tens]), (q_hbm, q_ref),
            (ck_hbm, ck_ref), (w_hbm, w_ref), (oc_hbm, oc_ref),
        ))
    ]
    for load in loads:
        load.start()
    stores = [
        pltpu.make_async_copy(src, dst, store_sem.at[i])
        for i, (src, dst) in enumerate((
            (gq_ref, gq_hbm), (gck_ref, gck_hbm), (gpk_ref, gpk_hbm), (gpv_ref, gpv_hbm),
            (gw_ref, gw_hbm),
        ))
    ]

    loads[0].wait()
    kall_ref[0, z * NYH + yh] = pk_ref[0]
    kall_ref[1, yh * NZ + z] = pk_ref[1]
    loads[1].wait()
    own_rows = ph_ref[...].astype(F32)
    for b in range(4):
        phs_ref[b * 4:(b + 1) * 4, :] = own_rows[:, b * 1024:(b + 1) * 1024]
    own_hp[...] = phs_ref[...].astype(BF16)
    hp_ref[tens] = own_hp[...]
    loads[2].wait()
    loads[3].wait()
    lane = lax.broadcasted_iota(jnp.int32, (8, 128), 1)
    own_scores = jnp.where(
        lane == 2 * cand, sc_ref[0, 0], jnp.where(lane == 2 * cand + 1, sc_ref[0, 1], 0.0)
    )
    s1_ref[yh] = own_scores
    for c in range(2):
        for r in range(4):
            base = c * 512 + r * 128
            qs_ref[base:base + 128, :] = q_ref[c, :, r * 128:(r + 1) * 128]
    dvp_ref[...] = jnp.zeros_like(dvp_ref)
    dvc_ref[...] = jnp.zeros_like(dvc_ref)
    dkp_ref[...] = jnp.zeros_like(dkp_ref)
    dkc_ref[...] = jnp.zeros_like(dkc_ref)
    for load in loads[4:]:
        load.wait()

    pl.semaphore_wait(barrier, (NT - 1) + (NZ - 1) + (NY - 1))

    def gather(own, whole, sems):
        a1 = Exchange(NYH, yh, at_yh, lambda p: own.at[0],
                      lambda s: whole.at[0, z * NYH + s], sems.at[0])
        b1 = Exchange(NZ, z, at_z, lambda p: own.at[1],
                      lambda s: whole.at[1, yh * NZ + s], sems.at[1])
        a2 = Exchange(NZ, z, at_z, lambda p: whole.at[0, pl.ds(z * NYH, NYH)],
                      lambda s: whole.at[0, pl.ds(s * NYH, NYH)], sems.at[2])
        b2 = Exchange(NYH, yh, at_yh, lambda p: whole.at[1, pl.ds(yh * NZ, NZ)],
                      lambda s: whole.at[1, pl.ds(s * NZ, NZ)], sems.at[3])
        return a1, b1, a2, b2

    hp_x = Exchange(NT, tens, at_t, lambda p: own_hp, lambda s: hp_ref.at[s], sem_hp)
    left, right = lax.rem(x + NX - 1, NX), lax.rem(x + 1, NX)
    across = lax.rem(x + 2, NX)

    def along(sem, block, rows, to):
        return pltpu.make_async_remote_copy(
            src_ref=hc_ref.at[block * 2 + core, rows],
            dst_ref=hc_ref.at[block * 2 + core, rows],
            send_sem=sem_hx.at[0, sem],
            recv_sem=sem_hx.at[1, sem],
            device_id=at_x(to),
            device_id_type=MESH,
        )

    both, upper, lower = pl.ds(0, 32), pl.ds(0, 16), pl.ds(16, 16)
    hc_sent = (
        along(0, x, both, right), along(1, x, both, left),
        along(2, left, upper, right), along(3, right, lower, left),
    )
    hc_came = (
        along(0, left, both, right), along(1, right, both, left),
        along(2, across, upper, right), along(3, across, lower, left),
    )
    s_1 = Exchange(NYH, yh, at_yh, lambda p: s1_ref.at[yh], lambda s: s1_ref.at[s], sem_s.at[0])
    s_2 = Exchange(NZ, z, at_z, lambda p: s2_ref.at[z], lambda s: s2_ref.at[s], sem_s.at[1])
    k_a1, k_b1, k_a2, k_b2 = gather(pk_ref, kall_ref, sem_k)

    def sibling(xx, mine):
        slot = xx * 2 + (core if mine else other)
        return pltpu.make_async_remote_copy(
            src_ref=hc_ref.at[xx * 2 + core],
            dst_ref=hc_ref.at[slot],
            send_sem=sem_hs.at[0, xx],
            recv_sem=sem_hs.at[1, xx],
            device_id=(dp, cand, x * 2 + other),
            device_id_type=MESH,
        )

    k_a1.start()
    k_b1.start()
    s_1.start()
    hp_x.start()
    hc_sent[0].start()
    hc_sent[1].start()
    sibling(x, True).start()

    k_a1.wait_recv()
    k_a2.start()
    k_b1.wait_recv()
    k_b2.start()
    s_1.wait_recv()
    s2_ref[z] = s1_ref[0] + s1_ref[1] + s1_ref[2] + s1_ref[3]
    s_2.start()

    hp_x.wait_recv()
    to = lax.broadcasted_iota(jnp.int32, (128, 128), 0)
    came = lax.broadcasted_iota(jnp.int32, (128, 128), 1)
    order = came == lax.rem(to // 4, 8) * 16 + (to // 32) * 4 + lax.rem(to, 4)
    hp_rows = dot(
        jnp.where(order, 1.0, 0.0).astype(BF16), hp_ref[...].reshape(128, 1024)
    ).astype(BF16)
    pv = jnp.zeros((32, HEAD), F32)
    for b in range(4):
        pv = pv + dot(hp_rows[b * 32:(b + 1) * 32], w_ref[b * 1024:(b + 1) * 1024, :])
    pv = pv.astype(BF16).reshape(2, 16, HEAD)
    vall_ref[0, z * NYH + yh] = pv[0]
    vall_ref[1, yh * NZ + z] = pv[1]

    class Own:
        def __init__(self, first, second):
            self.at = (first, second)

    v_a1, v_b1, v_a2, v_b2 = gather(
        Own(vall_ref.at[0, z * NYH + yh], vall_ref.at[1, yh * NZ + z]), vall_ref, sem_v
    )
    v_a1.start()
    v_b1.start()

    spot = lax.broadcasted_iota(jnp.int32, (1, 1024), 1)
    place = lax.rem(spot, 512)
    outer, inner, last = place // 128, lax.rem(place // 32, 4), lax.rem(spot, 32)
    wanted = jnp.where(
        spot < 512, outer * 256 + inner * 64 + last, inner * 256 + outer * 64 + 32 + last
    )
    sorted_hp = jnp.zeros((128, 1024), F32)
    for b in range(4):
        row = lax.broadcasted_iota(jnp.int32, (256, 1024), 0) + b * 256
        pick = jnp.where(row == wanted, 1.0, 0.0).astype(BF16)
        sorted_hp = sorted_hp + dot(hp_rows[:, b * 256:(b + 1) * 256], pick)
    sorted_hp = sorted_hp.astype(BF16)
    for d in range(2):
        for zh in range(2):
            rows = sorted_hp[(d * 2 + zh) * 32:(d * 2 + zh + 1) * 32]
            for j in range(4):
                sxa[zh * 4 + j, :, d * 128:(d + 1) * 128] = rows[:, j * 128:(j + 1) * 128]
                sxb[j * 2 + d, :, zh * 128:(zh + 1) * 128] = (
                    rows[:, 512 + j * 128:512 + (j + 1) * 128]
                )
    xa[z] = sxa[z]
    xb[y] = sxb[y]
    x_a = Exchange(NZ, z, at_z, lambda p: sxa.at[p], lambda s: xa.at[s], sem_x.at[0])
    x_b = Exchange(NY, y, at_y, lambda p: sxb.at[p], lambda s: xb.at[s], sem_x.at[1])
    x_a.start()
    x_b.start()

    for i, block in ((0, left), (1, right)):
        hc_came[i].wait_recv()
        hc_sent[i + 2].start()
        sibling(block, True).start()

    s_2.wait_recv()
    total = s2_ref[0]
    for i in range(1, NZ):
        total = total + s2_ref[i]
    list_grad = rank_gradient(total[0:1, 0:64], rk_ref[...])
    item = lax.broadcasted_iota(jnp.int32, (64, 1), 0)
    for c in range(2):
        own_grad = jnp.sum(
            jnp.where(item == 2 * cand + c, list_grad, 0.0), axis=0, keepdims=True
        )
        live = lax.broadcasted_iota(jnp.int32, (CAND, 128), 0) < ln_ref[0, c]
        for r in range(4):
            base = c * 512 + r * 128
            part = oc_ref[c, :, r * 128:(r + 1) * 128].astype(F32) * own_grad
            cs_ref[base:base + 128, :] = jnp.where(live, part, 0.0).astype(BF16)

    k_a2.wait_recv()
    k_b2.wait_recv()
    kt_ref[...] = kall_ref[...].reshape(PREFIX, HEAD).astype(F32).T.astype(BF16)

    def soft(n, carry):
        c = n // 2
        cols = pl.ds(pl.multiple_of(n * CHUNK, CHUNK), CHUNK)
        queries = qs_ref[cols, :]
        cot = cs_ref[cols, :]
        log_p = dot_nt(kall_ref[...].reshape(PREFIX, HEAD), queries)
        log_c = dot_nt(ck_ref[c], queries)
        slot = lax.broadcasted_iota(jnp.int32, (CAND, CHUNK), 0)
        position = lax.rem(lax.broadcasted_iota(jnp.int32, (CAND, CHUNK), 1), CAND)
        allowed = (slot <= position) & (slot < ln_ref[0, c])
        log_c = jnp.where(allowed, log_c, -jnp.inf)
        top = jnp.maximum(
            jnp.max(log_p, axis=0, keepdims=True), jnp.max(log_c, axis=0, keepdims=True)
        )
        exp_p = jnp.exp2((log_p - top) * EXP_SCALE)
        exp_c = jnp.exp2((log_c - top) * EXP_SCALE)
        inverse = 1.0 / (
            jnp.sum(exp_p, axis=0, keepdims=True) + jnp.sum(exp_c, axis=0, keepdims=True)
        )
        prob_p = exp_p * inverse
        prob_c = exp_c * inverse
        p_ref[0:PREFIX, cols] = prob_p
        p_ref[PREFIX:PREFIX + CAND, cols] = prob_c
        dvp_ref[...] += dot(prob_p.astype(BF16), cot)
        dvc_ref[c] += dot(prob_c.astype(BF16), cot)
        return carry

    lax.fori_loop(0, 1, soft, 0, unroll=True)
    lax.fori_loop(1, 2, soft, 0, unroll=True)
    v_a1.wait_recv()
    v_a2.start()
    v_b1.wait_recv()
    v_b2.start()
    hc_came[2].wait_recv()
    hc_came[3].wait_recv()
    sibling(across, True).start()
    lax.fori_loop(2, 4, soft, 0, unroll=True)

    def scatter(whole, ra1, rb1, ra2, rb2, ta2, tb2, sems, ny, my_y, at_group):
        a1 = Exchange(NZ, z, at_z, lambda p: whole.at[0, pl.ds(p * ny, ny)],
                      lambda s: ra1.at[s], sems.at[0])
        b1 = Exchange(ny, my_y, at_group, lambda p: whole.at[1, pl.ds(p * NZ, NZ)],
                      lambda s: rb1.at[s], sems.at[1])
        a2 = Exchange(ny, my_y, at_group, lambda p: ta2.at[p], lambda s: ra2.at[s], sems.at[2])
        b2 = Exchange(NZ, z, at_z, lambda p: tb2.at[p], lambda s: rb2.at[s], sems.at[3])

        def middle():
            a1.wait_recv()
            ra1[z] = whole[0, pl.ds(z * ny, ny)]
            total = ra1[0].astype(F32)
            for i in range(1, NZ):
                total = total + ra1[i].astype(F32)
            ta2[...] = total.astype(BF16)
            a2.start()
            b1.wait_recv()
            rb1[my_y] = whole[1, pl.ds(my_y * NZ, NZ)]
            total = rb1[0].astype(F32)
            for i in range(1, ny):
                total = total + rb1[i].astype(F32)
            tb2[...] = total.astype(BF16)
            b2.start()

        def end():
            a2.wait_recv()
            ra2[my_y] = ta2[my_y]
            first = ra2[0].astype(F32)
            for i in range(1, ny):
                first = first + ra2[i].astype(F32)
            b2.wait_recv()
            rb2[z] = tb2[z]
            second = rb2[0].astype(F32)
            for i in range(1, NZ):
                second = second + rb2[i].astype(F32)
            return first, second

        return (a1, b1, a2, b2), middle, end

    dv_all, dv_middle, dv_end = scatter(
        send_v, rva1, rvb1, rva2, rvb2, tva2, tvb2, sem_dv, NYH, yh, at_yh
    )
    send_v[...] = dvp_ref[...].astype(BF16).reshape(2, 32, 16, HEAD)
    dv_all[0].start()
    dv_all[1].start()

    def from_sibling(k, carry):
        sibling(k, False).wait_recv()
        return carry

    lax.fori_loop(0, NX, from_sibling, 0)
    for c in range(2):
        dvr_ref[:, c] = dvc_ref[c].reshape(8, 16, HEAD)
    dvr_t = dvr_ref[...].reshape(256, HEAD).T.astype(BF16)

    def weight(b, carry):
        cols = pl.ds(pl.multiple_of(b * 512, 512), 512)
        part = dot(dvr_t, hc_ref[:, :, cols].reshape(256, 512))
        rows = part.T.astype(BF16).reshape(2, NYH, 2, 32, HEAD)
        d, zz = b // 4, lax.rem(b, 4) * 2
        for i in range(2):
            for j in range(NYH):
                send_w[0, (zz + i) * NY + j * 2 + d] = rows[i, j, 0]
                send_w[1, (j * 2 + d) * NZ + zz + i] = rows[i, j, 1]
        return carry

    lax.fori_loop(0, 8, weight, 0)
    ring_a = Ring(z, at_z, send_w, 0, third_a, fourth_a, joined_a, came_a, sem_r.at[0])
    ring_b = Ring(y, at_y, send_w, 1, third_b, fourth_b, joined_b, came_b, sem_r.at[1])
    dw_a = Exchange(NY, y, at_y, lambda p: twa2.at[p], lambda s: rwa2.at[s], sem_dw.at[0])
    dw_b = Exchange(NZ, z, at_z, lambda p: twb2.at[p], lambda s: rwb2.at[s], sem_dw.at[1])
    ring_a.start()
    ring_b.start()
    dv_middle()

    cv = dot(hc_ref[...].reshape(256, WIDTH), w_ref[...]).astype(BF16).reshape(8, 2, 16, HEAD)
    for c in range(2):
        vc_ref[c] = cv[:, c].reshape(CAND, HEAD)
    v_a2.wait_recv()
    v_b2.wait_recv()

    def score(n, carry):
        c = n // 2
        cols = pl.ds(pl.multiple_of(n * CHUNK, CHUNK), CHUNK)
        queries = qs_ref[cols, :]
        cot = cs_ref[cols, :]
        dprob_p = dot_nt(vall_ref[...].reshape(PREFIX, HEAD), cot)
        dprob_c = dot_nt(vc_ref[c], cot)
        prob_p = p_ref[0:PREFIX, cols]
        prob_c = p_ref[PREFIX:PREFIX + CAND, cols]
        row_total = jnp.sum(prob_p * dprob_p, axis=0, keepdims=True) + jnp.sum(
            prob_c * dprob_c, axis=0, keepdims=True
        )
        ds_p = (prob_p * (dprob_p - row_total)).astype(BF16)
        ds_c = (prob_c * (dprob_c - row_total)).astype(BF16)
        dkp_ref[...] += dot(ds_p, queries)
        dkc_ref[c] += dot(ds_c, queries)
        kc_t = ck_ref[c].astype(F32).T.astype(BF16)
        gq_t = (dot(kt_ref[...], ds_p) + dot(kc_t, ds_c)) * INV_ROOT
        p_ref[0:128, cols] = gq_t
        return carry

    lax.fori_loop(0, 1, score, 0, unroll=True)
    ring_a.relay()
    ring_b.relay()
    lax.fori_loop(1, 2, score, 0, unroll=True)

    first, second = dv_end()
    gpv_ref[0] = first.astype(BF16)
    gpv_ref[1] = second.astype(BF16)
    stores[3].start()
    ga[z] = gpv_ref[...]
    gb[y] = gpv_ref[...]
    g_a = Exchange(NZ, z, at_z, lambda p: ga.at[z], lambda s: ga.at[s], sem_g.at[0])
    g_b = Exchange(NY, y, at_y, lambda p: gb.at[y], lambda s: gb.at[s], sem_g.at[1])
    g_a.start()
    g_b.start()
    lax.fori_loop(2, 4, score, 0, unroll=True)

    dk_all, dk_middle, dk_end = scatter(
        send_k, rka1, rkb1, rka2, rkb2, tka2, tkb2, sem_dk, NYH, yh, at_yh
    )
    send_k[...] = (dkp_ref[...] * INV_ROOT).astype(BF16).reshape(2, 32, 16, HEAD)
    dk_all[0].start()
    dk_all[1].start()

    for c in range(2):
        gck_ref[c] = (dkc_ref[c] * INV_ROOT).astype(BF16)
        for r in range(4):
            base = c * 512 + r * 128
            gq_ref[c, :, r * 128:(r + 1) * 128] = (
                p_ref[0:128, base:base + 128].T.astype(BF16)
            )
    stores[0].start()
    stores[1].start()

    x_a.wait_recv()
    x_b.wait_recv()

    def prefix_part(half):
        (g_a, g_b)[half].wait_recv()
        rows = (ga, gb)[half][...].reshape(256, HEAD).astype(F32).T.astype(BF16)
        part = dot(rows, (xa, xb)[half][...].reshape(256, 256))
        part = part.T
        if half == 0:
            part = part.reshape(2, NYH, 32, HEAD).swapaxes(0, 1)
        return part.reshape(8, 32, HEAD)

    twa2[...] = (ring_a.total() + prefix_part(0)).astype(BF16)
    dw_a.start()
    twb2[...] = (ring_b.total() + prefix_part(1)).astype(BF16)
    dw_b.start()
    dk_middle()
    first, second = dk_end()
    gpk_ref[0] = first.astype(BF16)
    gpk_ref[1] = second.astype(BF16)
    stores[2].start()
    for i, (one, mine, sent, came) in enumerate(((dw_a, y, twa2, rwa2), (dw_b, z, twb2, rwb2))):
        one.wait_recv()
        came[mine] = sent[mine]
        last = came[0].astype(F32)
        for j in range(1, 8):
            last = last + came[j].astype(F32)
        gw_ref[i * 32:(i + 1) * 32, :] = last
    stores[4].start()

    for group in (
        (*hc_sent, hp_x, s_1, s_2, k_a1, k_b1, k_a2, k_b2, v_a1, v_b1, v_a2, v_b2,
         x_a, x_b, g_a, g_b),
        (ring_a, ring_b, dw_a, dw_b), dv_all, dk_all,
    ):
        for one in group:
            one.wait_send()

    def sent(k, carry):
        sibling(k, True).wait_send()
        return carry

    lax.fori_loop(0, NX, sent, 0)
    for store in stores:
        store.wait()


def hand_over(*refs):
    sources, results, held, sems = refs[:5], refs[5:10], refs[10:15], refs[15]
    loads = [pltpu.make_async_copy(a, b, sems.at[0, i]) for i, (a, b) in enumerate(zip(sources, held))]
    stores = [pltpu.make_async_copy(a, b, sems.at[1, i]) for i, (a, b) in enumerate(zip(held, results))]
    for load in loads:
        load.start()
    for load, store in zip(loads, stores):
        load.wait()
        store.start()
    for store in stores:
        store.wait()


def shards(
    cand_query, cand_key, shared_prefix_key, cand_hidden, prefix_hidden, value_matrix,
    out_cotangent, cand_scores, ranking, lengths,
):
    vmem = pl.BlockSpec(memory_space=pltpu.VMEM)
    smem = pl.BlockSpec(memory_space=pltpu.SMEM)

    def small(count):
        return [
            pltpu.VMEM((NZ, count, 16, HEAD), BF16),
            pltpu.VMEM((count, NZ, 16, HEAD), BF16),
            pltpu.VMEM((count, 16, HEAD), BF16),
            pltpu.VMEM((NZ, 16, HEAD), BF16),
        ]

    hbm = pl.BlockSpec(memory_space=pltpu.HBM)
    ring_buffers = [
        pltpu.VMEM((2, 8, 32, HEAD), BF16),
        pltpu.VMEM((2, 4, 32, HEAD), BF16),
        pltpu.VMEM((2, 8, 32, HEAD), BF16),
        pltpu.VMEM((4, 8, 32, HEAD), BF16),
    ]
    shapes = (
        jax.ShapeDtypeStruct((2, CAND, 512), BF16),
        jax.ShapeDtypeStruct((2, CAND, HEAD), BF16),
        jax.ShapeDtypeStruct((2, 16, HEAD), BF16),
        jax.ShapeDtypeStruct((2, 16, HEAD), BF16),
        jax.ShapeDtypeStruct((64, HEAD), F32),
    )
    results = pl.pallas_call(
        kernel,
        out_shape=shapes,
        in_specs=[hbm] * 7 + [smem, vmem, smem],
        out_specs=(hbm,) * 5,
        scratch_shapes=[
            *(pltpu.VMEM(one.shape, one.dtype) for one in shapes),
            pltpu.SemaphoreType.DMA((5,)),
            pltpu.VMEM((2, CAND, 512), BF16),
            pltpu.VMEM((2, CAND, HEAD), BF16),
            pltpu.VMEM((2, 16, HEAD), BF16),
            pltpu.VMEM((4, WIDTH), BF16),
            pltpu.VMEM((WIDTH, HEAD), BF16),
            pltpu.VMEM((2, CAND, 512), BF16),
            pltpu.SemaphoreType.DMA((7,)),
            pltpu.VMEM((16, 1024), F32),
            pltpu.VMEM((16, 1024), BF16),
            pltpu.VMEM((NZ, 32, 256), BF16),
            pltpu.VMEM((NY, 32, 256), BF16),
            pltpu.VMEM((NZ, 32, 256), BF16),
            pltpu.VMEM((NY, 32, 256), BF16),
            pltpu.VMEM((NZ, 2, 16, HEAD), BF16),
            pltpu.VMEM((NY, 2, 16, HEAD), BF16),
            pltpu.VMEM((NT, 32, WIDTH), BF16),
            pltpu.VMEM((NT, 16, 1024), BF16),
            pltpu.VMEM((2, 32, 16, HEAD), BF16),
            pltpu.VMEM((2, 32, 16, HEAD), BF16),
            pltpu.VMEM((HEAD, PREFIX), BF16),
            pltpu.VMEM((NYH, 8, 128), F32),
            pltpu.VMEM((NZ, 8, 128), F32),
            pltpu.VMEM((1024, HEAD), BF16),
            pltpu.VMEM((1024, HEAD), BF16),
            pltpu.VMEM((PREFIX + CAND, 1024), F32),
            pltpu.VMEM((2, CAND, HEAD), BF16),
            pltpu.VMEM((PREFIX, HEAD), F32),
            pltpu.VMEM((2, CAND, HEAD), F32),
            pltpu.VMEM((PREFIX, HEAD), F32),
            pltpu.VMEM((2, CAND, HEAD), F32),
            pltpu.VMEM((8, 2, 16, HEAD), F32),
            pltpu.VMEM((2, 32, 16, HEAD), BF16),
            pltpu.VMEM((2, 32, 16, HEAD), BF16),
            *small(NYH),
            *small(NYH),
            pltpu.VMEM((NYH, 16, HEAD), BF16),
            pltpu.VMEM((NZ, 16, HEAD), BF16),
            pltpu.VMEM((NYH, 16, HEAD), BF16),
            pltpu.VMEM((NZ, 16, HEAD), BF16),
            pltpu.VMEM((2, 64, 32, HEAD), BF16),
            *ring_buffers,
            *ring_buffers,
            pltpu.VMEM((NY, 32, HEAD), BF16),
            pltpu.VMEM((NZ, 32, HEAD), BF16),
            pltpu.VMEM((NY, 32, HEAD), BF16),
            pltpu.VMEM((NZ, 32, HEAD), BF16),
            pltpu.SemaphoreType.DMA((2, NT)),
            pltpu.SemaphoreType.DMA((2, NX)),
            pltpu.SemaphoreType.DMA((2, NX)),
            pltpu.SemaphoreType.DMA((2, 2, NZ)),
            pltpu.SemaphoreType.DMA((4, 2, NZ)),
            pltpu.SemaphoreType.DMA((4, 2, NZ)),
            pltpu.SemaphoreType.DMA((4, 2, NZ)),
            pltpu.SemaphoreType.DMA((4, 2, NZ)),
            pltpu.SemaphoreType.DMA((4, 2, NZ)),
            pltpu.SemaphoreType.DMA((2, 2, NZ)),
            pltpu.SemaphoreType.DMA((2, 2, NZ)),
            pltpu.SemaphoreType.DMA((2, 2, NZ)),
        ],
        compiler_params=pltpu.CompilerParams(
            collective_id=0, has_side_effects=True, vmem_limit_bytes=64 * 1024 * 1024
        ),
    )(
        cand_query[0],
        cand_key[0],
        shared_prefix_key.reshape(2, 16, HEAD),
        cand_hidden.reshape(32, WIDTH),
        prefix_hidden[0],
        value_matrix,
        out_cotangent[0],
        cand_scores,
        ranking,
        lengths,
    )
    gq, gck, gpk, gpv, gw = pl.pallas_call(
        hand_over,
        out_shape=shapes,
        in_specs=[pl.BlockSpec(memory_space=pl.ANY)] * 5,
        out_specs=(hbm,) * 5,
        scratch_shapes=[
            *(pltpu.VMEM(one.shape, one.dtype) for one in shapes),
            pltpu.SemaphoreType.DMA((2, 5)),
        ],
        compiler_params=pltpu.CompilerParams(vmem_limit_bytes=64 * 1024 * 1024),
    )(*results)
    return (
        gq[None],
        gck[None],
        gpk.reshape(1, 32, HEAD),
        gpv.reshape(1, 32, HEAD),
        gw,
    )


def solution(mesh):
    placed = (
        P("dp", "cand", None, "tensor"),
        P("dp", "cand", None, "tensor"),
        P("dp", "cand", "tensor"),
        P("dp", "cand", "tensor", None),
        P("dp", ("cand", "tensor"), None),
        P(None, "tensor"),
        P("dp", "cand", None, "tensor"),
        P("dp", "cand"),
        P("dp", None),
        P("dp", "cand"),
    )
    return jax.shard_map(
        shards,
        mesh=mesh,
        in_specs=placed,
        out_specs=(
            P("dp", "cand", None, "tensor"),
            P("dp", "cand", None, "tensor"),
            P("dp", "cand", "tensor"),
            P("dp", "cand", "tensor"),
            P(("dp", "cand"), "tensor"),
        ),
        check_vma=False,
    )
```
